128 devices in a mesh: leaf: 8 (over x, core), panel: 16 (over z, y).
Axes of the slice: x: 4, y: 4, z: 4, core: 2. Of those that a mesh axis runs over, the one named last changes fastest.
Arguments:
- leaf_source: float32 [32, 16384], P(None, ('leaf', 'panel')), may hold values from -6 to 6
- leaf_noise: float32 [32, 16384], P(None, ('leaf', 'panel')), may hold values from -6 to 6
- sep_source: float32 [32, 16384], P(None, ('leaf', 'panel')), may hold values from -6 to 6
- sep_noise: float32 [32, 16384], P(None, ('leaf', 'panel')), may hold values from -6 to 6
- leaf_inverse: bfloat16 [8, 2048, 2048], P('leaf', 'panel'), may hold values from -0.125 to 0.125
- leaf_coupling: bfloat16 [8, 2048, 2048], P('leaf', 'panel'), may hold values from -0.0625 to 0.0625
- sep_inverse: bfloat16 [8, 2048, 2048], P('leaf', 'panel'), may hold values from -0.125 to 0.125
- sep_coupling: bfloat16 [8, 2048, 2048], P('leaf', 'panel'), may hold values from -0.0625 to 0.0625
- sep_length: int32 [8], P('leaf'), may hold values from 1024 to 2048, as said below
- leaf_map: int32 [8, 2048], P('leaf'), may hold values from 0 to 2047
- sep_map: int32 [8, 2048], P('leaf'), may hold values from 0 to 2047
Outputs:
- leaf_sample: float32 [32, 16384], P(None, ('leaf', 'panel'))
- sep_sample: float32 [32, 16384], P(None, ('leaf', 'panel'))
The draws below stay inside these ranges and needn't reach their ends.
Inputs may be any that keep to these rules, and one draw needn't show every extreme that they name: `sep_length`: some front has all 2048 rows live and another exactly half of them.
All inputs are finite; a program needn't handle non-finite values.
Results may differ from the reference program's by a relative error of at most 0.012.
Values may be sent and summed in bfloat16 or wider, within the bound.
A program may use at most 64 MiB of HBM per device.

```python
import jax
import jax.numpy as jnp
import numpy as np
from jax import lax

SAMPLES = 32
LEAF = 2048
SEP = 2048
LEVELS = 4
N_LEAF = 8


def draw_sep_length(key, part):
    key = jax.random.fold_in(key, 11)
    first_key, second_key, third_key = jax.random.split(key, 3)
    lengths = jax.random.randint(first_key, (N_LEAF,), SEP // 2, SEP + 1)
    chosen = jax.random.randint(second_key, (), 0, N_LEAF)
    other = (chosen + 1 + jax.random.randint(third_key, (), 0, N_LEAF - 1)) % N_LEAF
    lengths = lengths.at[chosen].set(SEP)
    lengths = lengths.at[other].set(SEP // 2)
    return lengths.astype(jnp.int32)


def touch_ends(drawn, stream_key, least, largest):
    dims = drawn.shape
    spot = [jax.random.randint(jax.random.fold_in(stream_key, axis), (), 0, dims[axis]) for axis in range(len(dims))]
    drawn = drawn.at[tuple(spot)].set(least)
    longest = dims.index(max(dims))
    spot[longest] = (spot[longest] + 1) % dims[longest]
    return drawn.at[tuple(spot)].set(largest)


def block_scale(rng, extent, cuts, smallest, high):
    def one(dim, blocks):
        draws = jax.random.uniform(jax.random.fold_in(jax.random.fold_in(rng, 6), dim), (blocks,), jnp.float32, smallest / len(cuts), high / len(cuts))
        return jnp.repeat(jnp.exp(draws), extent[dim] // blocks).reshape((-1,) + (1,) * (len(extent) - dim - 1))

    gain = one(*cuts[0])
    for cut in cuts[1:]:
        gain = gain * one(*cut)
    return gain


def normal_values(own_key, shape, deviation, reach, shards=(), kind=jnp.bfloat16):
    values = jax.random.normal(own_key, shape, jnp.float32) * deviation
    if len(shards) > 0:
        values = block_scale(own_key, shape, shards, -0.22, 0.18) * values
    return jnp.clip(values, min=-reach, max=reach).astype(kind)


def setup_inputs(seed: int = 0) -> dict:
    key_of = jax.random.split(jax.random.key(seed), 12)
    return {
        "leaf_source": normal_values(key_of[0], (SAMPLES, N_LEAF * LEAF), 1.0, 6.0, ((1, 128),), jnp.float32),
        "leaf_noise": normal_values(key_of[1], (SAMPLES, N_LEAF * LEAF), 1.0, 6.0, ((1, 128),), jnp.float32),
        "sep_source": normal_values(key_of[2], (SAMPLES, N_LEAF * SEP), 1.0, 6.0, ((1, 128),), jnp.float32),
        "sep_noise": normal_values(key_of[3], (SAMPLES, N_LEAF * SEP), 1.0, 6.0, ((1, 128),), jnp.float32),
        "leaf_inverse": normal_values(key_of[4], (N_LEAF, LEAF, LEAF), LEAF ** -0.5, 0.125, ((0, 8), (1, 16))),
        "leaf_coupling": normal_values(key_of[5], (N_LEAF, LEAF, SEP), (4 * LEAF) ** -0.5, 0.0625, ((0, 8), (1, 16))),
        "sep_inverse": normal_values(key_of[6], (N_LEAF, SEP, SEP), SEP ** -0.5, 0.125, ((0, 8), (1, 16))),
        "sep_coupling": normal_values(key_of[7], (N_LEAF, SEP, SEP), (4 * SEP) ** -0.5, 0.0625, ((0, 8), (1, 16))),
        "sep_length": draw_sep_length(jax.random.fold_in(key_of[11], 71), 0),
        "leaf_map": touch_ends(jax.random.randint(key_of[9], (N_LEAF, SEP), 0, SEP), jax.random.fold_in(key_of[9], 1), 0, SEP - 1).astype(jnp.int32),
        "sep_map": touch_ends(jax.random.randint(key_of[10], (N_LEAF, SEP), 0, SEP), jax.random.fold_in(key_of[10], 1), 0, SEP - 1).astype(jnp.int32),
    }


def tree_level(index):
    number = index + 1
    found = 1
    for bit_index in range(1, LEVELS):
        if number % (1 << bit_index) == 0:
            found += 1
    return found


def tree_parent(index, found):
    offset = 1 << (found - 1)
    if ((index + 1) // offset) % 4 == 1 or found == LEVELS - 1:
        return index + offset
    return index - offset


def spread(values, targets):
    blank_sum = jnp.zeros((values.shape[0], SEP), jnp.float32)
    return blank_sum.at[:, targets].add(values)


def by_block(array, size):
    return array.reshape(SAMPLES, N_LEAF, size).transpose(1, 0, 2)


def wide_dot(left, right):
    return jnp.dot(left.astype(jnp.float32), right.astype(jnp.float32), precision=lax.Precision.HIGHEST)


def reference(leaf_source, leaf_noise, sep_source, sep_noise, leaf_inverse, leaf_coupling, sep_inverse, sep_coupling, sep_length, leaf_map, sep_map):
    leaf_right = by_block(leaf_source, LEAF)
    leaf_extra = by_block(leaf_noise, LEAF)
    sep_right = by_block(sep_source, SEP)
    sep_extra = by_block(sep_noise, SEP)
    live_all = (jnp.arange(SEP, dtype=jnp.int32)[None, :] < sep_length[:, None]).astype(jnp.float32)[:, None, :]

    def leaf_forward(pieces):
        right_side, inverse, coupling, targets = pieces
        solved = wide_dot(right_side.astype(jnp.bfloat16), inverse)
        update = wide_dot(solved.astype(jnp.bfloat16), coupling)
        return solved, spread(update, targets)

    leaf_solved, leaf_spread = lax.map(leaf_forward, (leaf_right, leaf_inverse, leaf_coupling, leaf_map))
    leaf_parents = np.array([i - (i % 2) for i in range(N_LEAF)], dtype=np.int32)
    pending = jnp.zeros((N_LEAF, SAMPLES, SEP), jnp.float32).at[leaf_parents].add(leaf_spread)
    levels = [tree_level(i) for i in range(N_LEAF)]
    solved_all = jnp.zeros((N_LEAF, SAMPLES, SEP), jnp.float32)
    for section in range(1, LEVELS + 1):
        fronts = np.array([i for i in range(N_LEAF) if levels[i] == section], dtype=np.int32)
        live_rows = live_all[fronts]
        right_side = (live_rows * (sep_right[fronts] - pending[fronts])).astype(jnp.bfloat16)
        solved_now = live_rows * jnp.einsum("nks,nst->nkt", right_side.astype(jnp.float32), sep_inverse[fronts].astype(jnp.float32), precision=lax.Precision.HIGHEST)
        solved_all = solved_all.at[fronts].set(solved_now)
        if section < LEVELS:
            update = jnp.einsum("nks,nst->nkt", solved_now.astype(jnp.bfloat16).astype(jnp.float32), sep_coupling[fronts].astype(jnp.float32), precision=lax.Precision.HIGHEST)
            mapped = jax.vmap(spread)(update, sep_map[fronts])
            parents = np.array([tree_parent(int(i), section) for i in fronts], dtype=np.int32)
            pending = pending.at[parents].add(mapped)
    sample_all = jnp.zeros((N_LEAF, SAMPLES, SEP), jnp.float32)
    for section in range(LEVELS, 0, -1):
        fronts = np.array([i for i in range(N_LEAF) if levels[i] == section], dtype=np.int32)
        live_rows = live_all[fronts]
        if section < LEVELS:
            parents = np.array([tree_parent(int(i), section) for i in fronts], dtype=np.int32)
            parent_rows = sample_all[parents].astype(jnp.bfloat16)
            parent_view = jax.vmap(lambda rows_in, targets: rows_in[:, targets])(parent_rows, sep_map[fronts])
            correction = jnp.einsum("nkt,nst->nks", parent_view.astype(jnp.float32), sep_coupling[fronts].astype(jnp.float32), precision=lax.Precision.HIGHEST)
        else:
            correction = jnp.zeros_like(live_rows * sep_right[fronts])
        residual = (live_rows * (solved_all[fronts] + sep_extra[fronts] - correction)).astype(jnp.bfloat16)
        result = live_rows * jnp.einsum("nkt,nst->nks", residual.astype(jnp.float32), sep_inverse[fronts].astype(jnp.float32), precision=lax.Precision.HIGHEST)
        sample_all = sample_all.at[fronts].set(result)

    def leaf_backward(pieces):
        parent_rows, targets, coupling, inverse, solved, extra = pieces
        gathered = parent_rows[:, targets]
        correction = wide_dot(gathered, coupling.T)
        residual = (solved + extra - correction).astype(jnp.bfloat16)
        return wide_dot(residual, inverse.T)

    leaf_out = lax.map(leaf_backward, (sample_all[leaf_parents].astype(jnp.bfloat16), leaf_map, leaf_coupling, leaf_inverse, leaf_solved, leaf_extra))
    leaf_sample = leaf_out.transpose(1, 0, 2).reshape(SAMPLES, N_LEAF * LEAF)
    sep_sample = sample_all.transpose(1, 0, 2).reshape(SAMPLES, N_LEAF * SEP)
    return leaf_sample, sep_sample
```

```python
import jax
import jax.numpy as jnp
from jax import lax
from jax.experimental import pallas as pl
from jax.experimental.pallas import tpu as pltpu
from jax.sharding import PartitionSpec as P

MESH = pl.DeviceIdType.MESH
BF16 = jnp.bfloat16
F32 = jnp.float32
PANELS = 16
SIDE = 4
ROWS = 128
WIDTH = 2048
SAMPLES = 32
MAP_TILE = 256
PARTS = PANELS * 2


def nn(left, right):
    return jnp.dot(left, right, preferred_element_type=F32)


def nt(left, right):
    return lax.dot_general(left, right, (((1,), (1,)), ((), ())), preferred_element_type=F32)


def kernel(
    leaf_source,
    leaf_noise,
    sep_source,
    sep_noise,
    leaf_inverse,
    leaf_coupling,
    sep_inverse,
    sep_coupling,
    sep_length,
    leaf_map,
    sep_map,
    leaf_sample,
    sep_sample,
    leaf_mapped,
    sep_mapped,
    leaf_rs_out,
    leaf_rs_in,
    leaf_up_out,
    leaf_up_in,
    sep_rs_out,
    sep_rs_in,
    sep_up_out,
    sep_up_in,
    residual_in,
    parent_in,
    sample_out,
    leaf_parent_in,
    leaf_residual_in,
    send_sems,
    recv_sems,
):
    m = lax.axis_index("leaf")
    p = lax.axis_index("panel")
    z = lax.div(p, SIDE)
    y = lax.rem(p, SIDE)
    even = lax.rem(m, 2) == 0
    second = lax.rem(m, 4) == 1
    third = m == 3
    top = m == 7
    inner = jnp.logical_or(second, third)
    rows = [lax.rem(z + step, SIDE) * SIDE for step in range(SIDE)]
    columns = [lax.rem(y + step, SIDE) for step in range(SIDE)]
    order = [(2, 2), (2, 1), (2, 3), (1, 2), (3, 2), (1, 1), (1, 3), (3, 1), (3, 3)]
    order += [(0, 2), (2, 0), (0, 1), (0, 3), (1, 0), (3, 0)]
    others = [rows[dz] + columns[dy] for dz, dy in order]
    everyone = others + [p]

    def copy(source, target, kind, leaf, panel):
        pltpu.make_async_remote_copy(
            src_ref=source,
            dst_ref=target,
            send_sem=send_sems.at[kind],
            recv_sem=recv_sems.at[kind],
            device_id=(leaf, panel),
            device_id_type=MESH,
        ).start()

    def await_parts(sem, count):
        span = leaf_up_in.at[pl.ds(0, count)]
        pltpu.make_async_copy(span, span, sem).wait()

    def scatter(value, out, into, base, kind, leaf, own):
        for q in range(PANELS):
            out[q] = value[:, q * ROWS : (q + 1) * ROWS].astype(BF16)
        for q in others:
            copy(out.at[q], into.at[base + p], kind, leaf, q)
        if own:
            into[base + p] = out[p]
        else:
            copy(out.at[p], into.at[base + p], kind, leaf, p)

    def total(into, first, count):
        summed = into[first].astype(F32)
        for index in range(first + 1, first + count):
            summed = summed + into[index].astype(F32)
        return summed

    def whole(into):
        return jnp.concatenate([into[index] for index in range(PANELS)], axis=1)

    def publish(share, into, kind):
        into[p] = share
        for q in others:
            copy(into.at[p], into.at[p], kind, m, q)

    def mapped(coupling, targets, out):
        def body(tile, carry):
            first = pl.multiple_of(tile * MAP_TILE, MAP_TILE)
            parent_row = lax.broadcasted_iota(jnp.int32, (MAP_TILE, WIDTH), 0) + first
            chosen = jnp.where(parent_row == targets[...], 1.0, 0.0).astype(BF16)
            out[:, pl.ds(first, MAP_TILE)] = nt(coupling[0], chosen).astype(BF16)
            return carry

        lax.fori_loop(0, WIDTH // MAP_TILE, body, 0)

    barrier = pltpu.get_barrier_semaphore()

    def greet(leaf):
        for q in everyone:
            pl.semaphore_signal(barrier, inc=1, device_id=(leaf, q), device_id_type=MESH)

    for q in others:
        pl.semaphore_signal(barrier, inc=1, device_id=(m, q), device_id_type=MESH)

    @pl.when(even)
    def _():
        greet(m + 1)

    @pl.when(jnp.logical_not(even))
    def _():
        greet(m - 1)

    @pl.when(lax.rem(m, 4) == 2)
    def _():
        greet(m - 1)

    @pl.when(second)
    def _():
        greet(m + 1)
        greet(3)

    @pl.when(third)
    def _():
        greet(1)
        greet(5)
        greet(7)

    @pl.when(top)
    def _():
        greet(3)

    leaf_partial = nn(leaf_source[...].astype(BF16), leaf_inverse[0])

    @pl.when(lax.rem(m, 4) == 0)
    def _():
        pl.semaphore_wait(barrier, 15 + 16)

    @pl.when(jnp.logical_or(lax.rem(m, 4) == 2, top))
    def _():
        pl.semaphore_wait(barrier, 15 + 32)

    @pl.when(second)
    def _():
        pl.semaphore_wait(barrier, 15 + 48)

    @pl.when(third)
    def _():
        pl.semaphore_wait(barrier, 15 + 64)

    scatter(leaf_partial, leaf_rs_out, leaf_rs_in, 0, 0, m, True)
    mapped(leaf_coupling, leaf_map, leaf_mapped)
    await_parts(recv_sems.at[0], 15)
    leaf_solved = total(leaf_rs_in, 0, PANELS)
    leaf_update = nn(leaf_solved.astype(BF16), leaf_mapped[...])

    @pl.when(even)
    def _():
        scatter(leaf_update, leaf_up_out, leaf_up_in, 0, 1, m, True)

    @pl.when(jnp.logical_not(even))
    def _():
        scatter(leaf_update, leaf_up_out, leaf_up_in, PANELS, 1, m - 1, False)

    mapped(sep_coupling, sep_map, sep_mapped)
    lane = lax.broadcasted_iota(jnp.int32, (1, ROWS), 1) + p * ROWS
    live = jnp.where(lane < sep_length[0], 1.0, 0.0)

    def front_forward(pending):
        right_side = (live * (sep_source[...] - pending)).astype(BF16)
        scatter(nn(right_side, sep_inverse[0]), sep_rs_out, sep_rs_in, 0, 2, m, True)

    @pl.when(even)
    def _():
        await_parts(recv_sems.at[1], 31)
        front_forward(total(leaf_up_in, 0, 32))

    @pl.when(inner)
    def _():
        await_parts(recv_sems.at[3], 32)
        front_forward(total(sep_up_in, 0, 32))

    @pl.when(top)
    def _():
        await_parts(recv_sems.at[3], 16)
        front_forward(total(sep_up_in, 0, 16))

    await_parts(recv_sems.at[2], 15)
    sep_solved = live * total(sep_rs_in, 0, PANELS)
    parent = jnp.where(third, 7, jnp.where(m == 1, 3, jnp.where(m == 5, 3, jnp.where(lax.rem(m, 4) == 0, m + 1, m - 1))))
    child = jnp.where(jnp.logical_or(m == 5, lax.rem(m, 4) == 2), PANELS, 0)

    @pl.when(jnp.logical_not(top))
    def _():
        update = nn(sep_solved.astype(BF16), sep_mapped[...])
        scatter(update, sep_up_out, sep_up_in, child, 3, parent, False)

    sep_wanted = sep_solved + sep_noise[...]

    @pl.when(jnp.logical_not(top))
    def _():
        await_parts(recv_sems.at[4], 16)
        correction = nt(whole(parent_in), sep_mapped[...])
        publish((live * (sep_wanted - correction)).astype(BF16), residual_in, 5)

    @pl.when(top)
    def _():
        publish((live * sep_wanted).astype(BF16), residual_in, 5)

    await_parts(recv_sems.at[5], 15)
    sample = live * nt(whole(residual_in), sep_inverse[0])
    sample_out[...] = sample.astype(BF16)

    def descend(leaf, into, kind):
        for q in everyone:
            copy(sample_out, into.at[p], kind, leaf, q)

    @pl.when(top)
    def _():
        descend(3, parent_in, 4)

    @pl.when(third)
    def _():
        descend(1, parent_in, 4)
        descend(5, parent_in, 4)

    @pl.when(second)
    def _():
        descend(m - 1, parent_in, 4)
        descend(m + 1, parent_in, 4)

    @pl.when(even)
    def _():
        leaf_parent_in[p] = sample_out[...]
        for q in others:
            copy(sample_out, leaf_parent_in.at[p], 6, m, q)
        descend(m + 1, leaf_parent_in, 6)

    sep_sample[...] = sample

    @pl.when(even)
    def _():
        await_parts(recv_sems.at[6], 15)

    @pl.when(jnp.logical_not(even))
    def _():
        await_parts(recv_sems.at[6], 16)

    leaf_correction = nt(whole(leaf_parent_in), leaf_mapped[...])
    leaf_residual = (leaf_solved + leaf_noise[...] - leaf_correction).astype(BF16)
    publish(leaf_residual, leaf_residual_in, 7)
    await_parts(recv_sems.at[7], 15)
    leaf_sample[...] = nt(whole(leaf_residual_in), leaf_inverse[0])

    for kind in (0, 2, 5, 7):
        await_parts(send_sems.at[kind], 15)

    @pl.when(even)
    def _():
        await_parts(send_sems.at[1], 15)
        await_parts(send_sems.at[6], 31)

    @pl.when(jnp.logical_not(even))
    def _():
        await_parts(send_sems.at[1], 16)

    @pl.when(jnp.logical_not(top))
    def _():
        await_parts(send_sems.at[3], 16)

    @pl.when(inner)
    def _():
        await_parts(send_sems.at[4], 32)

    @pl.when(top)
    def _():
        await_parts(send_sems.at[4], 16)


def shards(*arrays):
    vmem = pl.BlockSpec(memory_space=pltpu.VMEM)
    share = jax.ShapeDtypeStruct((SAMPLES, ROWS), F32)
    slots = pltpu.VMEM((PANELS, SAMPLES, ROWS), BF16)
    pair = pltpu.VMEM((2 * PANELS, SAMPLES, ROWS), BF16)
    slab = pltpu.VMEM((ROWS, WIDTH), BF16)
    one = pltpu.VMEM((SAMPLES, ROWS), BF16)
    return pl.pallas_call(
        kernel,
        out_shape=(share, share),
        in_specs=[vmem] * 8 + [pl.BlockSpec(memory_space=pltpu.SMEM)] + [vmem] * 2,
        out_specs=(vmem, vmem),
        scratch_shapes=[slab, slab]
        + [slots, slots, slots, pair]
        + [slots, slots, slots, pair]
        + [slots, slots, one, slots, slots]
        + [pltpu.SemaphoreType.DMA((8,)), pltpu.SemaphoreType.DMA((8,))],
        compiler_params=pltpu.CompilerParams(
            collective_id=0, has_side_effects=True, vmem_limit_bytes=32 * 1024 * 1024
        ),
    )(*arrays)


def solution(mesh):
    in_specs = (
        P(None, ("leaf", "panel")),
        P(None, ("leaf", "panel")),
        P(None, ("leaf", "panel")),
        P(None, ("leaf", "panel")),
        P("leaf", "panel", None),
        P("leaf", "panel", None),
        P("leaf", "panel", None),
        P("leaf", "panel", None),
        P("leaf"),
        P("leaf", None),
        P("leaf", None),
    )
    out_specs = (P(None, ("leaf", "panel")), P(None, ("leaf", "panel")))
    return jax.shard_map(shards, mesh=mesh, in_specs=in_specs, out_specs=out_specs, check_vma=False)
```

```python
import jax
import jax.numpy as jnp
from jax import lax
from jax.experimental import pallas as pl
from jax.experimental.pallas import tpu as pltpu
from jax.sharding import PartitionSpec as P

MESH = pl.DeviceIdType.MESH
BF16 = jnp.bfloat16
F32 = jnp.float32
PANELS = 16
SIDE = 4
ROWS = 128
WIDTH = 2048
SAMPLES = 32
MAP_TILE = 256
PARTS = PANELS * 2


def nn(left, right):
    return jnp.dot(left, right, preferred_element_type=F32)


def nt(left, right):
    return lax.dot_general(left, right, (((1,), (1,)), ((), ())), preferred_element_type=F32)


def kernel(
    leaf_source_hbm,
    leaf_noise_hbm,
    sep_source_hbm,
    sep_noise_hbm,
    leaf_inverse_hbm,
    leaf_coupling_hbm,
    sep_inverse_hbm,
    sep_coupling_hbm,
    sep_length,
    leaf_map_hbm,
    sep_map_hbm,
    leaf_sample,
    sep_sample,
    leaf_source,
    leaf_noise,
    sep_source,
    sep_noise,
    leaf_inverse,
    leaf_coupling,
    sep_inverse,
    sep_coupling,
    leaf_map,
    sep_map,
    load_sems,
    leaf_mapped,
    sep_mapped,
    leaf_rs_out,
    leaf_rs_in,
    leaf_up_out,
    leaf_up_in,
    sep_rs_out,
    sep_rs_in,
    sep_up_out,
    sep_up_in,
    residual_in,
    parent_in,
    sample_out,
    leaf_parent_in,
    leaf_residual_in,
    send_sems,
    recv_sems,
):
    loads = [
        pltpu.make_async_copy(source, target, load_sems.at[index])
        for index, (source, target) in enumerate(
            (
                (leaf_source_hbm, leaf_source),
                (leaf_inverse_hbm, leaf_inverse),
                (leaf_map_hbm, leaf_map),
                (leaf_coupling_hbm, leaf_coupling),
                (sep_map_hbm, sep_map),
                (sep_coupling_hbm, sep_coupling),
                (sep_source_hbm, sep_source),
                (sep_inverse_hbm, sep_inverse),
                (sep_noise_hbm, sep_noise),
                (leaf_noise_hbm, leaf_noise),
            )
        )
    ]
    for load in loads:
        load.start()
    m = lax.axis_index("leaf")
    p = lax.axis_index("panel")
    z = lax.div(p, SIDE)
    y = lax.rem(p, SIDE)
    even = lax.rem(m, 2) == 0
    second = lax.rem(m, 4) == 1
    third = m == 3
    top = m == 7
    inner = jnp.logical_or(second, third)
    rows = [lax.rem(z + step, SIDE) * SIDE for step in range(SIDE)]
    columns = [lax.rem(y + step, SIDE) for step in range(SIDE)]
    order = [(2, 2), (2, 1), (2, 3), (1, 2), (3, 2), (1, 1), (1, 3), (3, 1), (3, 3)]
    order += [(0, 2), (2, 0), (0, 1), (0, 3), (1, 0), (3, 0)]
    others = [rows[dz] + columns[dy] for dz, dy in order]
    everyone = others + [p]

    def copy(source, target, kind, leaf, panel):
        pltpu.make_async_remote_copy(
            src_ref=source,
            dst_ref=target,
            send_sem=send_sems.at[kind],
            recv_sem=recv_sems.at[kind],
            device_id=(leaf, panel),
            device_id_type=MESH,
        ).start()

    def await_parts(sem, count):
        span = leaf_up_in.at[pl.ds(0, count)]
        pltpu.make_async_copy(span, span, sem).wait()

    def scatter(value, out, into, base, kind, leaf, own):
        for q in range(PANELS):
            out[q] = value[:, q * ROWS : (q + 1) * ROWS].astype(BF16)
        for q in others:
            copy(out.at[q], into.at[base + p], kind, leaf, q)
        if own:
            into[base + p] = out[p]
        else:
            copy(out.at[p], into.at[base + p], kind, leaf, p)

    def total(into, first, count):
        summed = into[first].astype(F32)
        for index in range(first + 1, first + count):
            summed = summed + into[index].astype(F32)
        return summed

    def whole(into):
        return jnp.concatenate([into[index] for index in range(PANELS)], axis=1)

    def publish(share, into, kind):
        into[p] = share
        for q in others:
            copy(into.at[p], into.at[p], kind, m, q)

    def mapped(coupling, targets, out):
        def body(tile, carry):
            first = pl.multiple_of(tile * MAP_TILE, MAP_TILE)
            parent_row = lax.broadcasted_iota(jnp.int32, (MAP_TILE, WIDTH), 0) + first
            chosen = jnp.where(parent_row == targets[...], 1.0, 0.0).astype(BF16)
            out[:, pl.ds(first, MAP_TILE)] = nt(coupling[0], chosen).astype(BF16)
            return carry

        lax.fori_loop(0, WIDTH // MAP_TILE, body, 0)

    barrier = pltpu.get_barrier_semaphore()

    def greet(leaf):
        for q in everyone:
            pl.semaphore_signal(barrier, inc=1, device_id=(leaf, q), device_id_type=MESH)

    for q in others:
        pl.semaphore_signal(barrier, inc=1, device_id=(m, q), device_id_type=MESH)

    @pl.when(even)
    def _():
        greet(m + 1)

    @pl.when(jnp.logical_not(even))
    def _():
        greet(m - 1)

    @pl.when(lax.rem(m, 4) == 2)
    def _():
        greet(m - 1)

    @pl.when(second)
    def _():
        greet(m + 1)
        greet(3)

    @pl.when(third)
    def _():
        greet(1)
        greet(5)
        greet(7)

    @pl.when(top)
    def _():
        greet(3)

    for load in loads:
        load.wait()
    leaf_partial = nn(leaf_source[...].astype(BF16), leaf_inverse[0])

    @pl.when(lax.rem(m, 4) == 0)
    def _():
        pl.semaphore_wait(barrier, 15 + 16)

    @pl.when(jnp.logical_or(lax.rem(m, 4) == 2, top))
    def _():
        pl.semaphore_wait(barrier, 15 + 32)

    @pl.when(second)
    def _():
        pl.semaphore_wait(barrier, 15 + 48)

    @pl.when(third)
    def _():
        pl.semaphore_wait(barrier, 15 + 64)

    scatter(leaf_partial, leaf_rs_out, leaf_rs_in, 0, 0, m, True)
    mapped(leaf_coupling, leaf_map, leaf_mapped)
    await_parts(recv_sems.at[0], 15)
    leaf_solved = total(leaf_rs_in, 0, PANELS)
    leaf_update = nn(leaf_solved.astype(BF16), leaf_mapped[...])

    @pl.when(even)
    def _():
        scatter(leaf_update, leaf_up_out, leaf_up_in, 0, 1, m, True)

    @pl.when(jnp.logical_not(even))
    def _():
        scatter(leaf_update, leaf_up_out, leaf_up_in, PANELS, 1, m - 1, False)

    mapped(sep_coupling, sep_map, sep_mapped)
    lane = lax.broadcasted_iota(jnp.int32, (1, ROWS), 1) + p * ROWS
    live = jnp.where(lane < sep_length[0], 1.0, 0.0)

    def front_forward(pending):
        right_side = (live * (sep_source[...] - pending)).astype(BF16)
        scatter(nn(right_side, sep_inverse[0]), sep_rs_out, sep_rs_in, 0, 2, m, True)

    @pl.when(even)
    def _():
        await_parts(recv_sems.at[1], 31)
        front_forward(total(leaf_up_in, 0, 32))

    @pl.when(inner)
    def _():
        await_parts(recv_sems.at[3], 32)
        front_forward(total(sep_up_in, 0, 32))

    @pl.when(top)
    def _():
        await_parts(recv_sems.at[3], 16)
        front_forward(total(sep_up_in, 0, 16))

    await_parts(recv_sems.at[2], 15)
    sep_solved = live * total(sep_rs_in, 0, PANELS)
    parent = jnp.where(third, 7, jnp.where(m == 1, 3, jnp.where(m == 5, 3, jnp.where(lax.rem(m, 4) == 0, m + 1, m - 1))))
    child = jnp.where(jnp.logical_or(m == 5, lax.rem(m, 4) == 2), PANELS, 0)

    @pl.when(jnp.logical_not(top))
    def _():
        update = nn(sep_solved.astype(BF16), sep_mapped[...])
        scatter(update, sep_up_out, sep_up_in, child, 3, parent, False)

    sep_wanted = sep_solved + sep_noise[...]

    @pl.when(jnp.logical_not(top))
    def _():
        await_parts(recv_sems.at[4], 16)
        correction = nt(whole(parent_in), sep_mapped[...])
        publish((live * (sep_wanted - correction)).astype(BF16), residual_in, 5)

    @pl.when(top)
    def _():
        publish((live * sep_wanted).astype(BF16), residual_in, 5)

    await_parts(recv_sems.at[5], 15)
    sample = live * nt(whole(residual_in), sep_inverse[0])
    sample_out[...] = sample.astype(BF16)

    def descend(leaf, into, kind):
        for q in everyone:
            copy(sample_out, into.at[p], kind, leaf, q)

    @pl.when(top)
    def _():
        descend(3, parent_in, 4)

    @pl.when(third)
    def _():
        descend(1, parent_in, 4)
        descend(5, parent_in, 4)

    @pl.when(second)
    def _():
        descend(m - 1, parent_in, 4)
        descend(m + 1, parent_in, 4)

    @pl.when(even)
    def _():
        leaf_parent_in[p] = sample_out[...]
        for q in others:
            copy(sample_out, leaf_parent_in.at[p], 6, m, q)
        descend(m + 1, leaf_parent_in, 6)

    sep_sample[...] = sample

    @pl.when(even)
    def _():
        await_parts(recv_sems.at[6], 15)

    @pl.when(jnp.logical_not(even))
    def _():
        await_parts(recv_sems.at[6], 16)

    leaf_correction = nt(whole(leaf_parent_in), leaf_mapped[...])
    leaf_residual = (leaf_solved + leaf_noise[...] - leaf_correction).astype(BF16)
    publish(leaf_residual, leaf_residual_in, 7)
    await_parts(recv_sems.at[7], 15)
    leaf_sample[...] = nt(whole(leaf_residual_in), leaf_inverse[0])

    for kind in (0, 2, 5, 7):
        await_parts(send_sems.at[kind], 15)

    @pl.when(even)
    def _():
        await_parts(send_sems.at[1], 15)
        await_parts(send_sems.at[6], 31)

    @pl.when(jnp.logical_not(even))
    def _():
        await_parts(send_sems.at[1], 16)

    @pl.when(jnp.logical_not(top))
    def _():
        await_parts(send_sems.at[3], 16)

    @pl.when(inner)
    def _():
        await_parts(send_sems.at[4], 32)

    @pl.when(top)
    def _():
        await_parts(send_sems.at[4], 16)


def shards(*arrays):
    vmem = pl.BlockSpec(memory_space=pltpu.VMEM)
    hbm = pl.BlockSpec(memory_space=pltpu.HBM)
    share = jax.ShapeDtypeStruct((SAMPLES, ROWS), F32)
    vector = pltpu.VMEM((SAMPLES, ROWS), F32)
    block = pltpu.VMEM((1, ROWS, WIDTH), BF16)
    targets = pltpu.VMEM((1, WIDTH), jnp.int32)
    slots = pltpu.VMEM((PANELS, SAMPLES, ROWS), BF16)
    pair = pltpu.VMEM((2 * PANELS, SAMPLES, ROWS), BF16)
    slab = pltpu.VMEM((ROWS, WIDTH), BF16)
    one = pltpu.VMEM((SAMPLES, ROWS), BF16)
    return pl.pallas_call(
        kernel,
        out_shape=(share, share),
        in_specs=[hbm] * 8 + [pl.BlockSpec(memory_space=pltpu.SMEM)] + [hbm] * 2,
        out_specs=(vmem, vmem),
        scratch_shapes=[vector] * 4
        + [block] * 4
        + [targets] * 2
        + [pltpu.SemaphoreType.DMA((10,))]
        + [slab, slab]
        + [slots, slots, slots, pair]
        + [slots, slots, slots, pair]
        + [slots, slots, one, slots, slots]
        + [pltpu.SemaphoreType.DMA((8,)), pltpu.SemaphoreType.DMA((8,))],
        compiler_params=pltpu.CompilerParams(
            collective_id=0, has_side_effects=True, vmem_limit_bytes=48 * 1024 * 1024
        ),
    )(*arrays)


def solution(mesh):
    in_specs = (
        P(None, ("leaf", "panel")),
        P(None, ("leaf", "panel")),
        P(None, ("leaf", "panel")),
        P(None, ("leaf", "panel")),
        P("leaf", "panel", None),
        P("leaf", "panel", None),
        P("leaf", "panel", None),
        P("leaf", "panel", None),
        P("leaf"),
        P("leaf", None),
        P("leaf", None),
    )
    out_specs = (P(None, ("leaf", "panel")), P(None, ("leaf", "panel")))
    return jax.shard_map(shards, mesh=mesh, in_specs=in_specs, out_specs=out_specs, check_vma=False)
```

```python
import jax
import jax.numpy as jnp
from jax import lax
from jax.experimental import pallas as pl
from jax.experimental.pallas import tpu as pltpu
from jax.sharding import PartitionSpec as P

MESH = pl.DeviceIdType.MESH
BF16 = jnp.bfloat16
F32 = jnp.float32
PANELS = 16
SIDE = 4
ROWS = 128
WIDTH = 2048
SAMPLES = 32
MAP_TILE = 256
PARTS = PANELS * 2


def nn(left, right):
    return jnp.dot(left, right, preferred_element_type=F32)


def nt(left, right):
    return lax.dot_general(left, right, (((1,), (1,)), ((), ())), preferred_element_type=F32)


def kernel(
    leaf_source_hbm,
    leaf_noise_hbm,
    sep_source_hbm,
    sep_noise_hbm,
    leaf_inverse_hbm,
    leaf_coupling_hbm,
    sep_inverse_hbm,
    sep_coupling_hbm,
    sep_length,
    leaf_map_hbm,
    sep_map_hbm,
    leaf_sample,
    sep_sample,
    leaf_source,
    leaf_noise,
    sep_source,
    sep_noise,
    leaf_inverse,
    leaf_coupling,
    sep_inverse,
    sep_coupling,
    leaf_map,
    sep_map,
    load_sems,
    leaf_mapped,
    sep_mapped,
    leaf_rs_out,
    leaf_rs_in,
    leaf_up_out,
    leaf_up_in,
    sep_rs_out,
    sep_rs_in,
    sep_up_out,
    sep_up_in,
    residual_in,
    parent_in,
    sample_out,
    leaf_parent_in,
    leaf_residual_in,
    send_sems,
    recv_sems,
):
    loads = [
        pltpu.make_async_copy(source, target, load_sems.at[index])
        for index, (source, target) in enumerate(
            (
                (leaf_source_hbm, leaf_source),
                (leaf_inverse_hbm, leaf_inverse),
                (leaf_map_hbm, leaf_map),
                (leaf_coupling_hbm, leaf_coupling),
                (sep_map_hbm, sep_map),
                (sep_coupling_hbm, sep_coupling),
                (sep_source_hbm, sep_source),
                (sep_inverse_hbm, sep_inverse),
                (sep_noise_hbm, sep_noise),
                (leaf_noise_hbm, leaf_noise),
            )
        )
    ]
    for load in loads:
        load.start()
    m = lax.axis_index("leaf")
    p = lax.axis_index("panel")
    z = lax.div(p, SIDE)
    y = lax.rem(p, SIDE)
    even = lax.rem(m, 2) == 0
    second = lax.rem(m, 4) == 1
    third = m == 3
    top = m == 7
    inner = jnp.logical_or(second, third)
    rows = [lax.rem(z + step, SIDE) * SIDE for step in range(SIDE)]
    columns = [lax.rem(y + step, SIDE) for step in range(SIDE)]
    order = [(2, 2), (2, 1), (2, 3), (1, 2), (3, 2), (1, 1), (1, 3), (3, 1), (3, 3)]
    order += [(0, 2), (2, 0), (0, 1), (0, 3), (1, 0), (3, 0)]
    others = [rows[dz] + columns[dy] for dz, dy in order]
    everyone = others + [p]

    def copy(source, target, kind, leaf, panel):
        pltpu.make_async_remote_copy(
            src_ref=source,
            dst_ref=target,
            send_sem=send_sems.at[kind],
            recv_sem=recv_sems.at[kind],
            device_id=(leaf, panel),
            device_id_type=MESH,
        ).start()

    def await_parts(sem, count):
        span = leaf_up_in.at[pl.ds(0, count)]
        pltpu.make_async_copy(span, span, sem).wait()

    def scatter(value, out, into, base, kind, leaf, own):
        for q in range(PANELS):
            out[q] = value[:, q * ROWS : (q + 1) * ROWS].astype(BF16)
        for q in others:
            copy(out.at[q], into.at[base + p], kind, leaf, q)
        if own:
            into[base + p] = out[p]
        else:
            copy(out.at[p], into.at[base + p], kind, leaf, p)

    def total(into, first, count):
        summed = into[first].astype(F32)
        for index in range(first + 1, first + count):
            summed = summed + into[index].astype(F32)
        return summed

    def whole(into):
        return jnp.concatenate([into[index] for index in range(PANELS)], axis=1)

    def publish(share, into, kind):
        into[p] = share
        for q in others:
            copy(into.at[p], into.at[p], kind, m, q)

    def mapped(coupling, targets, out):
        def body(tile, carry):
            first = pl.multiple_of(tile * MAP_TILE, MAP_TILE)
            parent_row = lax.broadcasted_iota(jnp.int32, (MAP_TILE, WIDTH), 0) + first
            chosen = jnp.where(parent_row == targets[...], 1.0, 0.0).astype(BF16)
            out[:, pl.ds(first, MAP_TILE)] = nt(coupling[0], chosen).astype(BF16)
            return carry

        lax.fori_loop(0, WIDTH // MAP_TILE, body, 0)

    barrier = pltpu.get_barrier_semaphore()

    def greet(leaf):
        for q in everyone:
            pl.semaphore_signal(barrier, inc=1, device_id=(leaf, q), device_id_type=MESH)

    for q in others:
        pl.semaphore_signal(barrier, inc=1, device_id=(m, q), device_id_type=MESH)

    @pl.when(even)
    def _():
        greet(m + 1)

    @pl.when(jnp.logical_not(even))
    def _():
        greet(m - 1)

    @pl.when(lax.rem(m, 4) == 2)
    def _():
        greet(m - 1)

    @pl.when(second)
    def _():
        greet(m + 1)
        greet(3)

    @pl.when(third)
    def _():
        greet(1)
        greet(5)
        greet(7)

    @pl.when(top)
    def _():
        greet(3)

    for load in loads:
        load.wait()
    leaf_partial = nn(leaf_source[...].astype(BF16), leaf_inverse[0])

    @pl.when(lax.rem(m, 4) == 0)
    def _():
        pl.semaphore_wait(barrier, 15 + 16)

    @pl.when(jnp.logical_or(lax.rem(m, 4) == 2, top))
    def _():
        pl.semaphore_wait(barrier, 15 + 32)

    @pl.when(second)
    def _():
        pl.semaphore_wait(barrier, 15 + 48)

    @pl.when(third)
    def _():
        pl.semaphore_wait(barrier, 15 + 64)

    scatter(leaf_partial, leaf_rs_out, leaf_rs_in, 0, 0, m, True)
    mapped(leaf_coupling, leaf_map, leaf_mapped)
    await_parts(recv_sems.at[0], 15)
    leaf_solved = total(leaf_rs_in, 0, PANELS)
    leaf_update = nn(leaf_solved.astype(BF16), leaf_mapped[...])

    @pl.when(even)
    def _():
        scatter(leaf_update, leaf_up_out, leaf_up_in, 0, 1, m, True)

    @pl.when(jnp.logical_not(even))
    def _():
        scatter(leaf_update, leaf_up_out, leaf_up_in, PANELS, 1, m - 1, False)

    mapped(sep_coupling, sep_map, sep_mapped)
    lane = lax.broadcasted_iota(jnp.int32, (1, ROWS), 1) + p * ROWS
    live = jnp.where(lane < sep_length[0], 1.0, 0.0)

    def front_forward(pending):
        right_side = (live * (sep_source[...] - pending)).astype(BF16)
        scatter(nn(right_side, sep_inverse[0]), sep_rs_out, sep_rs_in, 0, 2, m, True)

    @pl.when(even)
    def _():
        await_parts(recv_sems.at[1], 31)
        front_forward(total(leaf_up_in, 0, 32))

    @pl.when(inner)
    def _():
        await_parts(recv_sems.at[3], 32)
        front_forward(total(sep_up_in, 0, 32))

    @pl.when(top)
    def _():
        await_parts(recv_sems.at[3], 16)
        front_forward(total(sep_up_in, 0, 16))

    await_parts(recv_sems.at[2], 15)
    sep_solved = live * total(sep_rs_in, 0, PANELS)
    parent = jnp.where(third, 7, jnp.where(m == 1, 3, jnp.where(m == 5, 3, jnp.where(lax.rem(m, 4) == 0, m + 1, m - 1))))
    child = jnp.where(jnp.logical_or(m == 5, lax.rem(m, 4) == 2), PANELS, 0)

    @pl.when(jnp.logical_not(top))
    def _():
        update = nn(sep_solved.astype(BF16), sep_mapped[...])
        scatter(update, sep_up_out, sep_up_in, child, 3, parent, False)

    sep_wanted = sep_solved + sep_noise[...]

    @pl.when(jnp.logical_not(top))
    def _():
        await_parts(recv_sems.at[4], 16)
        correction = nt(whole(parent_in), sep_mapped[...])
        publish((live * (sep_wanted - correction)).astype(BF16), residual_in, 5)

    @pl.when(top)
    def _():
        publish((live * sep_wanted).astype(BF16), residual_in, 5)

    await_parts(recv_sems.at[5], 15)
    sample = live * nt(whole(residual_in), sep_inverse[0])
    sample_out[...] = sample.astype(BF16)

    def descend(leaf, into, kind):
        for q in everyone:
            copy(sample_out, into.at[p], kind, leaf, q)

    @pl.when(top)
    def _():
        descend(3, parent_in, 4)

    @pl.when(third)
    def _():
        descend(1, parent_in, 4)
        descend(5, parent_in, 4)

    @pl.when(second)
    def _():
        descend(m - 1, parent_in, 4)
        descend(m + 1, parent_in, 4)

    @pl.when(even)
    def _():
        leaf_parent_in[p] = sample_out[...]
        for q in others:
            copy(sample_out, leaf_parent_in.at[p], 6, m, q)
        descend(m + 1, leaf_parent_in, 6)

    sep_sample[...] = sample

    @pl.when(even)
    def _():
        await_parts(recv_sems.at[6], 15)

    @pl.when(jnp.logical_not(even))
    def _():
        await_parts(recv_sems.at[6], 16)

    leaf_correction = nt(whole(leaf_parent_in), leaf_mapped[...])
    leaf_residual = (leaf_solved + leaf_noise[...] - leaf_correction).astype(BF16)
    publish(leaf_residual, leaf_residual_in, 7)
    await_parts(recv_sems.at[7], 15)
    leaf_sample[...] = nt(whole(leaf_residual_in), leaf_inverse[0])

    for kind in (0, 2, 5, 7):
        await_parts(send_sems.at[kind], 15)

    @pl.when(even)
    def _():
        await_parts(send_sems.at[1], 15)
        await_parts(send_sems.at[6], 31)

    @pl.when(jnp.logical_not(even))
    def _():
        await_parts(send_sems.at[1], 16)

    @pl.when(jnp.logical_not(top))
    def _():
        await_parts(send_sems.at[3], 16)

    @pl.when(inner)
    def _():
        await_parts(send_sems.at[4], 32)

    @pl.when(top)
    def _():
        await_parts(send_sems.at[4], 16)


def shards(*arrays):
    vmem = pl.BlockSpec(memory_space=pltpu.VMEM)
    hbm = pl.BlockSpec(memory_space=pltpu.HBM)
    share = jax.ShapeDtypeStruct((SAMPLES, ROWS), F32)
    vector = pltpu.VMEM((SAMPLES, ROWS), F32)
    block = pltpu.VMEM((1, ROWS, WIDTH), BF16)
    targets = pltpu.VMEM((1, WIDTH), jnp.int32)
    slots = pltpu.VMEM((PANELS, SAMPLES, ROWS), BF16)
    pair = pltpu.VMEM((2 * PANELS, SAMPLES, ROWS), BF16)
    slab = pltpu.VMEM((ROWS, WIDTH), BF16)
    one = pltpu.VMEM((SAMPLES, ROWS), BF16)
    return pl.pallas_call(
        kernel,
        out_shape=(share, share),
        in_specs=[hbm] * 8 + [pl.BlockSpec(memory_space=pltpu.SMEM)] + [hbm] * 2,
        out_specs=(vmem, vmem),
        scratch_shapes=[vector] * 4
        + [block] * 4
        + [targets] * 2
        + [pltpu.SemaphoreType.DMA((10,))]
        + [slab, slab]
        + [slots, slots, slots, pair]
        + [slots, slots, slots, pair]
        + [slots, slots, one, slots, slots]
        + [pltpu.SemaphoreType.DMA((8,)), pltpu.SemaphoreType.DMA((8,))],
        compiler_params=pltpu.CompilerParams(
            collective_id=0, has_side_effects=True, vmem_limit_bytes=60 * 1024 * 1024
        ),
    )(*arrays)


def solution(mesh):
    in_specs = (
        P(None, ("leaf", "panel")),
        P(None, ("leaf", "panel")),
        P(None, ("leaf", "panel")),
        P(None, ("leaf", "panel")),
        P("leaf", "panel", None),
        P("leaf", "panel", None),
        P("leaf", "panel", None),
        P("leaf", "panel", None),
        P("leaf"),
        P("leaf", None),
        P("leaf", None),
    )
    out_specs = (P(None, ("leaf", "panel")), P(None, ("leaf", "panel")))
    return jax.shard_map(shards, mesh=mesh, in_specs=in_specs, out_specs=out_specs, check_vma=False)
```

```python
import jax
import jax.numpy as jnp
from jax import lax
from jax.experimental import pallas as pl
from jax.experimental.pallas import tpu as pltpu
from jax.sharding import PartitionSpec as P

MESH = pl.DeviceIdType.MESH
BF16 = jnp.bfloat16
F32 = jnp.float32
PANELS = 16
SIDE = 4
ROWS = 128
GROUP = SIDE * ROWS
WIDTH = 2048
SAMPLES = 32
PART = 8
MAP_TILE = 256
LEAF_RS, LEAF_UP, SEP_RS, SEP_UP, DOWN, OUT, LEAF_DOWN, LEAF_RES = range(8)
NOISE, SOURCE, WANTED, M_NEAR, M_FAR, I_TURN, I_NEAR, I_FAR, L_NEAR, L_FAR = range(8, 18)
KINDS = 18


def nn(left, right):
    return jnp.dot(left, right, preferred_element_type=F32)


def nt(left, right):
    return lax.dot_general(left, right, (((1,), (1,)), ((), ())), preferred_element_type=F32)


def fold(value):
    half = value.shape[1] // 2
    return jnp.concatenate([value[:, :half], value[:, half:]], axis=0)


def unfold(value):
    return jnp.concatenate([value[:PART], value[PART:]], axis=1)


def total(into, first, count):
    summed = into[first].astype(F32)
    for index in range(first + 1, first + count):
        summed = summed + into[index].astype(F32)
    return summed


def kernel(
    leaf_source_hbm,
    leaf_noise_hbm,
    sep_source_hbm,
    sep_noise_hbm,
    leaf_inverse_hbm,
    leaf_coupling_hbm,
    sep_inverse_hbm,
    sep_coupling_hbm,
    sep_length,
    leaf_map_hbm,
    sep_map_hbm,
    leaf_sample,
    sep_sample,
    leaf_source,
    leaf_noise,
    sep_source,
    sep_noise,
    leaf_inverse,
    leaf_coupling,
    sep_inverse,
    sep_coupling,
    leaf_map,
    sep_map,
    load_sems,
    sep_rows,
    leaf_rows,
    turned,
    sep_columns,
    leaf_rs_out,
    leaf_rs_in,
    leaf_up_out,
    leaf_up_in,
    sep_rs_out,
    sep_rs_in,
    sep_up_out,
    sep_up_in,
    down_out,
    down_in,
    out_out,
    out_in,
    leaf_down_in,
    leaf_residual_in,
    source_in,
    noise_in,
    wanted_out,
    wanted_in,
    solved,
    send_sems,
    recv_sems,
):
    loads = [
        pltpu.make_async_copy(source, target, load_sems.at[index])
        for index, (source, target) in enumerate(
            (
                (leaf_source_hbm, leaf_source),
                (leaf_inverse_hbm, leaf_inverse),
                (sep_map_hbm, sep_map),
                (sep_coupling_hbm, sep_coupling),
                (sep_inverse_hbm, sep_inverse),
                (leaf_map_hbm, leaf_map),
                (leaf_coupling_hbm, leaf_coupling),
                (sep_source_hbm, sep_source),
                (sep_noise_hbm, sep_noise),
                (leaf_noise_hbm, leaf_noise),
            )
        )
    ]
    for load in loads:
        load.start()
    m = lax.axis_index("leaf")
    p = lax.axis_index("panel")
    z = lax.div(p, SIDE)
    y = lax.rem(p, SIDE)
    core = lax.rem(m, 2)
    even = core == 0
    odd = core == 1
    second = lax.rem(m, 4) == 1
    third = m == 3
    top = m == 7
    s = jnp.where(even, z, y)
    g = jnp.where(even, y, z)

    def place(parity, split, group):
        return split * (4 - 3 * parity) + group * (1 + 3 * parity)

    def step(value, by):
        return lax.rem(value + by, SIDE)

    zs = [step(z, by) * SIDE for by in range(SIDE)]
    ys = [step(y, by) for by in range(SIDE)]
    order = [(2, 2), (2, 1), (2, 3), (1, 2), (3, 2), (1, 1), (1, 3), (3, 1), (3, 3)]
    order += [(0, 2), (2, 0), (0, 1), (0, 3), (1, 0), (3, 0)]
    others = [zs[dz] + ys[dy] for dz, dy in order]

    def copy(source, target, kind, leaf, panel):
        pltpu.make_async_remote_copy(
            src_ref=source,
            dst_ref=target,
            send_sem=send_sems.at[kind],
            recv_sem=recv_sems.at[kind],
            device_id=(leaf, panel),
            device_id_type=MESH,
        ).start()

    spans = {4: source_in, 8: leaf_up_in, 32: sep_up_in, 128: sep_columns, 512: sep_rows}

    def settle(sem, size, count):
        span = spans[size].at[pl.ds(0, count)]
        pltpu.make_async_copy(span, span, sem).wait()

    def arrive(kind, size, count):
        settle(recv_sems.at[kind], size, count)

    def mapped(coupling, targets, out, slot):
        def body(tile, carry):
            first = pl.multiple_of(tile * MAP_TILE, MAP_TILE)
            parent_row = lax.broadcasted_iota(jnp.int32, (MAP_TILE, WIDTH), 0) + first
            chosen = jnp.where(parent_row == targets[...], 1.0, 0.0).astype(BF16)
            out[slot, :, pl.ds(first, MAP_TILE)] = nt(coupling[0], chosen).astype(BF16)
            return carry

        lax.fori_loop(0, WIDTH // MAP_TILE, body, 0)

    barrier = pltpu.get_barrier_semaphore()

    def greet(leaf, panel):
        pl.semaphore_signal(barrier, inc=1, device_id=(leaf, panel), device_id_type=MESH)

    def greet_front(leaf, parity):
        for group in range(SIDE):
            greet(leaf, place(parity, s, group))

    twin = m + 1 - 2 * core
    for q in others:
        greet(m, q)
    for q in others + [p]:
        greet(twin, q)

    @pl.when(lax.rem(m, 4) == 2)
    def _():
        greet_front(m - 1, 1)

    @pl.when(second)
    def _():
        greet_front(m + 1, 0)
        greet_front(3, 1)

    @pl.when(third)
    def _():
        greet_front(1, 1)
        greet_front(5, 1)
        greet_front(7, 1)

    @pl.when(top)
    def _():
        greet_front(3, 1)

    for load in loads[:2]:
        load.wait()
    leaf_partial = nn(leaf_source[...].astype(BF16), leaf_inverse[0])
    for q in range(PANELS):
        leaf_rs_out[q] = leaf_partial[:, q * ROWS : (q + 1) * ROWS].astype(BF16)
    leaf_rs_in[p] = leaf_rs_out[p]
    for load in loads[2:4]:
        load.wait()
    mapped(sep_coupling, sep_map, sep_rows, s)
    for load in loads[4:]:
        load.wait()

    @pl.when(even)
    def _():
        for group in range(SIDE):
            for k in range(SIDE):
                first = (k * SIDE + group) * ROWS
                turned[group, :, k * ROWS : (k + 1) * ROWS] = sep_inverse[0, :, first : first + ROWS]

    @pl.when(odd)
    def _():
        for group in range(SIDE):
            turned[group] = sep_inverse[0, :, group * GROUP : (group + 1) * GROUP]

    sep_columns[p] = turned[g]
    noise_in[s] = sep_noise[pl.ds(pl.multiple_of(s * PART, PART), PART), :]
    source_in[p] = sep_source[pl.ds(pl.multiple_of(s * PART, PART), PART), :]

    def rows_near(first, count):
        for by in (1, 3):
            copy(
                sep_rows.at[s, pl.ds(first, count)],
                sep_rows.at[s, pl.ds(first, count)],
                M_NEAR,
                m,
                place(core, step(s, by), g),
            )

    def rows_far():
        arrive(M_NEAR, 512, 2)
        for by, first in ((1, 0), (3, ROWS // 2)):
            slot = step(s, 4 - by)
            part = sep_rows.at[slot, pl.ds(first, ROWS // 2)]
            copy(part, part, M_FAR, m, place(core, step(s, by), g))

    def columns_turn():
        for by in (2, 1, 3):
            group = step(g, by)
            copy(turned.at[group], sep_columns.at[p], I_TURN, m, place(core, s, group))

    def columns_near():
        arrive(I_TURN, 128, 3)
        for group in range(SIDE):
            for by in (1, 3):
                part = sep_columns.at[place(core, s, group)]
                copy(part, part, I_NEAR, m, place(core, step(s, by), g))

    def columns_far():
        arrive(I_NEAR, 128, 8)
        for by, first in ((1, 0), (3, 2)):
            for group in (first, first + 1):
                part = sep_columns.at[place(core, step(s, 4 - by), group)]
                copy(part, part, I_FAR, m, place(core, step(s, by), g))

    def leaf_rows_near():
        for by in (1, 3):
            copy(leaf_rows.at[z], leaf_rows.at[z], L_NEAR, m, zs[by] + y)

    def leaf_rows_far():
        copy(leaf_rows.at[z], leaf_rows.at[z], L_FAR, m, zs[2] + y)

    @pl.when(lax.rem(m, 4) == 0)
    def _():
        pl.semaphore_wait(barrier, 31)

    @pl.when(jnp.logical_or(lax.rem(m, 4) == 2, top))
    def _():
        pl.semaphore_wait(barrier, 35)

    @pl.when(second)
    def _():
        pl.semaphore_wait(barrier, 39)

    @pl.when(third)
    def _():
        pl.semaphore_wait(barrier, 43)

    for q in others:
        copy(leaf_rs_out.at[q], leaf_rs_in.at[p], LEAF_RS, m, q)
    for by in (2, 1, 3):
        there = step(s, by)
        part = sep_noise.at[pl.ds(pl.multiple_of(there * PART, PART), PART)]
        copy(part, noise_in.at[s], NOISE, m, place(core, there, g))

    @pl.when(odd)
    def _():
        for dz, dy in order:
            part = sep_source.at[pl.ds(pl.multiple_of(ys[dy] * PART, PART), PART)]
            copy(part, source_in.at[p], SOURCE, m, zs[dz] + ys[dy])
        columns_turn()
        rows_near(0, ROWS)

    @pl.when(even)
    def _():
        rows_near(0, ROWS // 2)

    mapped(leaf_coupling, leaf_map, leaf_rows, z)
    arrive(LEAF_RS, 8, 15)
    leaf_solved = total(leaf_rs_in, 0, PANELS)
    leaf_update = nn(leaf_solved.astype(BF16), leaf_rows[z])
    for q in range(PANELS):
        leaf_up_out[q] = leaf_update[:, q * ROWS : (q + 1) * ROWS].astype(BF16)

    @pl.when(even)
    def _():
        for q in others:
            copy(leaf_up_out.at[q], leaf_up_in.at[p], LEAF_UP, m, q)
        leaf_up_in[p] = leaf_up_out[p]
        rows_near(ROWS // 2, ROWS // 2)

    @pl.when(odd)
    def _():
        for q in others + [p]:
            copy(leaf_up_out.at[q], leaf_up_in.at[PANELS + p], LEAF_UP, m - 1, q)

    wanted_out[...] = leaf_solved + leaf_noise[...]
    wanted_in[z] = wanted_out[pl.ds(pl.multiple_of(z * PART, PART), PART), :]
    for by in (2, 1, 3):
        part = wanted_out.at[pl.ds(pl.multiple_of(step(z, by) * PART, PART), PART)]
        copy(part, wanted_in.at[z], WANTED, m, zs[by] + y)

    length = sep_length[0]
    lane = lax.broadcasted_iota(jnp.int32, (1, ROWS), 1)
    live_own = jnp.where(lane + p * ROWS < length, 1.0, 0.0)
    live_group = jnp.concatenate(
        [jnp.where(lane + place(core, k, g) * ROWS < length, 1.0, 0.0) for k in range(SIDE)], axis=1
    )
    live_all = jnp.where(lax.broadcasted_iota(jnp.int32, (1, WIDTH), 1) < length, 1.0, 0.0)

    @pl.when(even)
    def _():
        arrive(LEAF_UP, 8, 31)
        pending = total(leaf_up_in, 0, 2 * PANELS)
        right_side = (live_own * (sep_source[...] - pending)).astype(BF16)
        partial = nn(right_side, sep_inverse[0])
        for split in range(SIDE):
            rows = partial[split * PART : (split + 1) * PART]
            for group in range(SIDE):
                firsts = [(k * SIDE + group) * ROWS for k in range(SIDE)]
                chunk = jnp.concatenate([rows[:, first : first + ROWS] for first in firsts], axis=1)
                sep_rs_out[split * SIDE + group] = fold(chunk).astype(BF16)
        for q in others:
            copy(sep_rs_out.at[q], sep_rs_in.at[p], SEP_RS, m, q)
        sep_rs_in[p] = sep_rs_out[p]
        rows_far()
        arrive(SEP_RS, 8, 15)
        solved[...] = live_group * unfold(total(sep_rs_in, 0, PANELS))

    def front_forward(count):
        pending = unfold(total(sep_up_in, 0, count))
        source = jnp.concatenate([source_in[q] for q in range(PANELS)], axis=1)
        right_side = (live_all * (source - pending)).astype(BF16)
        solved[...] = live_group * nn(right_side, sep_columns[...].reshape(WIDTH, GROUP))

    @pl.when(odd)
    def _():
        columns_near()
        rows_far()
        columns_far()
        leaf_rows_near()
        arrive(SOURCE, 4, 15)
        arrive(I_FAR, 128, 4)

    @pl.when(jnp.logical_or(second, third))
    def _():
        arrive(SEP_UP, 32, 8)
        front_forward(8)

    @pl.when(top)
    def _():
        arrive(SEP_UP, 32, 4)
        front_forward(4)

    arrive(M_FAR, 512, 1)
    first_child = jnp.logical_or(lax.rem(m, 4) == 0, jnp.logical_or(m == 1, third))
    slot = jnp.where(first_child, 0, SIDE) + g
    low_parent = jnp.where(lax.rem(m, 4) == 0, m + 1, m - 1)
    parent = jnp.where(third, 7, jnp.where(even, low_parent, 3))

    @pl.when(jnp.logical_not(top))
    def _():
        update = nn(solved[...].astype(BF16), sep_rows[...].reshape(GROUP, WIDTH))
        sep_up_out[...] = fold(update).astype(BF16)
        for group in range(SIDE):
            copy(sep_up_out, sep_up_in.at[slot], SEP_UP, parent, place(1, s, group))

    @pl.when(even)
    def _():
        columns_turn()
        columns_near()
        leaf_rows_near()
        leaf_rows_far()
        columns_far()
        arrive(I_FAR, 128, 4)

    @pl.when(jnp.logical_and(odd, jnp.logical_not(top)))
    def _():
        leaf_rows_far()

    arrive(NOISE, 4, 3)
    noise = jnp.concatenate([noise_in[k] for k in range(SIDE)], axis=1)

    @pl.when(jnp.logical_not(top))
    def _():
        arrive(DOWN, 32, 4)
        view = unfold(total(down_in, 0, SIDE)).astype(BF16)
        solved[...] = solved[...] - nt(view, sep_rows[...].reshape(GROUP, WIDTH))

    residual = (live_group * (solved[...] + noise)).astype(BF16)
    partial_sample = live_all * nt(residual, sep_columns[...].reshape(WIDTH, GROUP))
    down_out[...] = fold(partial_sample).astype(BF16)

    def descend(leaf, parity):
        for group in range(SIDE):
            copy(down_out, down_in.at[g], DOWN, leaf, place(parity, s, group))

    @pl.when(top)
    def _():
        descend(3, 1)
        leaf_rows_far()

    @pl.when(third)
    def _():
        descend(1, 1)
        descend(5, 1)

    @pl.when(second)
    def _():
        descend(m - 1, 0)
        descend(m + 1, 0)

    @pl.when(even)
    def _():
        for by in (2, 1, 3):
            copy(down_out, leaf_down_in.at[y], LEAF_DOWN, m, zs[0] + ys[by])
        for by in (2, 1, 3, 0):
            copy(down_out, leaf_down_in.at[y], LEAF_DOWN, m + 1, zs[0] + ys[by])
        leaf_down_in[y] = down_out[...]

    for q in range(PANELS):
        out_out[q] = partial_sample[:, q * ROWS : (q + 1) * ROWS]
    for q in others:
        copy(out_out.at[q], out_in.at[p], OUT, m, q)
    out_in[p] = out_out[p]
    arrive(L_NEAR, 512, 2)
    arrive(L_FAR, 512, 1)
    arrive(WANTED, 4, 3)

    @pl.when(even)
    def _():
        arrive(LEAF_DOWN, 32, 3)

    @pl.when(odd)
    def _():
        arrive(LEAF_DOWN, 32, 4)

    leaf_view = unfold(total(leaf_down_in, 0, SIDE)).astype(BF16)
    correction = nt(leaf_view, leaf_rows[...].reshape(GROUP, WIDTH))
    wanted = jnp.concatenate([wanted_in[k] for k in range(SIDE)], axis=1)
    leaf_residual_in[p] = fold(wanted - correction).astype(BF16)
    for q in others:
        copy(leaf_residual_in.at[p], leaf_residual_in.at[p], LEAF_RES, m, q)
    arrive(OUT, 4, 15)
    for split in range(SIDE):
        if_even = total(out_in, split * SIDE, SIDE)
        if_odd = out_in[split] + out_in[split + 4] + out_in[split + 8] + out_in[split + 12]
        sep_sample[split * PART : (split + 1) * PART, :] = jnp.where(even, if_even, if_odd)
    arrive(LEAF_RES, 8, 15)
    pieces = [unfold(leaf_residual_in[q].astype(F32)) for q in range(PANELS)]
    blocks = []
    for q in range(PANELS):
        k, group = q // SIDE, q % SIDE
        cut = [pieces[split * SIDE + group][:, k * ROWS : (k + 1) * ROWS] for split in range(SIDE)]
        blocks.append(jnp.concatenate(cut, axis=0).astype(BF16))
    leaf_sample[...] = nt(jnp.concatenate(blocks, axis=1), leaf_inverse[0])

    def sent(kind, size, count):
        settle(send_sems.at[kind], size, count)

    sent(LEAF_RS, 8, 15)
    sent(OUT, 4, 15)
    sent(LEAF_RES, 8, 15)
    sent(NOISE, 4, 3)
    sent(WANTED, 4, 3)
    sent(M_NEAR, 512, 2)
    sent(M_FAR, 512, 1)
    sent(I_TURN, 128, 3)
    sent(I_NEAR, 128, 8)
    sent(I_FAR, 128, 4)
    sent(L_NEAR, 512, 2)
    sent(L_FAR, 512, 1)

    @pl.when(even)
    def _():
        sent(LEAF_UP, 8, 15)
        sent(SEP_RS, 8, 15)
        sent(LEAF_DOWN, 32, 7)

    @pl.when(odd)
    def _():
        sent(LEAF_UP, 8, 16)
        sent(SOURCE, 4, 15)

    @pl.when(jnp.logical_not(top))
    def _():
        sent(SEP_UP, 32, 4)

    @pl.when(jnp.logical_or(second, third))
    def _():
        sent(DOWN, 32, 8)

    @pl.when(top)
    def _():
        sent(DOWN, 32, 4)


def shards(*arrays):
    vmem = pl.BlockSpec(memory_space=pltpu.VMEM)
    hbm = pl.BlockSpec(memory_space=pl.ANY)
    share = jax.ShapeDtypeStruct((SAMPLES, ROWS), F32)
    vector = pltpu.VMEM((SAMPLES, ROWS), F32)
    block = pltpu.VMEM((1, ROWS, WIDTH), BF16)
    targets = pltpu.VMEM((1, WIDTH), jnp.int32)
    slots = pltpu.VMEM((PANELS, SAMPLES, ROWS), BF16)
    split = pltpu.VMEM((PANELS, 2 * PART, GROUP // 2), BF16)
    rows = pltpu.VMEM((SIDE, ROWS, WIDTH), BF16)
    partial = (2 * PART, WIDTH // 2)
    pieces = pltpu.VMEM((PANELS, PART, ROWS), F32)
    ring = pltpu.VMEM((SIDE, PART, ROWS), F32)
    return pl.pallas_call(
        kernel,
        out_shape=(share, share),
        in_specs=[hbm] * 8 + [pl.BlockSpec(memory_space=pltpu.SMEM)] + [hbm] * 2,
        out_specs=(vmem, vmem),
        scratch_shapes=[vector] * 4
        + [block] * 4
        + [targets] * 2
        + [pltpu.SemaphoreType.DMA((10,))]
        + [rows, rows]
        + [pltpu.VMEM((SIDE, ROWS, GROUP), BF16), pltpu.VMEM((PANELS, ROWS, GROUP), BF16)]
        + [slots, slots, slots, pltpu.VMEM((2 * PANELS, SAMPLES, ROWS), BF16)]
        + [split, split]
        + [pltpu.VMEM(partial, BF16), pltpu.VMEM((2 * SIDE,) + partial, BF16)]
        + [pltpu.VMEM(partial, BF16), pltpu.VMEM((SIDE,) + partial, BF16)]
        + [pieces, pieces]
        + [pltpu.VMEM((SIDE,) + partial, BF16), split]
        + [pieces, ring, vector, ring, pltpu.VMEM((PART, GROUP), F32)]
        + [pltpu.SemaphoreType.DMA((KINDS,)), pltpu.SemaphoreType.DMA((KINDS,))],
        compiler_params=pltpu.CompilerParams(
            collective_id=0, has_side_effects=True, vmem_limit_bytes=60 * 1024 * 1024
        ),
    )(*arrays)


def solution(mesh):
    in_specs = (
        P(None, ("leaf", "panel")),
        P(None, ("leaf", "panel")),
        P(None, ("leaf", "panel")),
        P(None, ("leaf", "panel")),
        P("leaf", "panel", None),
        P("leaf", "panel", None),
        P("leaf", "panel", None),
        P("leaf", "panel", None),
        P("leaf"),
        P("leaf", None),
        P("leaf", None),
    )
    out_specs = (P(None, ("leaf", "panel")), P(None, ("leaf", "panel")))
    return jax.shard_map(shards, mesh=mesh, in_specs=in_specs, out_specs=out_specs, check_vma=False)
```

```python
import jax
import jax.numpy as jnp
from jax import lax
from jax.experimental import pallas as pl
from jax.experimental.pallas import tpu as pltpu
from jax.sharding import PartitionSpec as P

MESH = pl.DeviceIdType.MESH
BF16 = jnp.bfloat16
F32 = jnp.float32
PANELS = 16
SIDE = 4
ROWS = 128
GROUP = SIDE * ROWS
WIDTH = 2048
SAMPLES = 32
PART = 8
MAP_TILE = 256
HALVES = 4
HALF = WIDTH // HALVES
LEAF_RS, LEAF_UP, SEP_RS, LOW_UP, OUT, LEAF_RES, NOISE, SOURCE, WANTED, SEP_RES, SAMPLE = range(11)
M_NEAR, M_FAR, I_TURN, I_NEAR, I_FAR = range(11, 16)
SEP_UP, DOWN = range(16, 24, HALVES)
KINDS = 24


def nn(left, right):
    return jnp.dot(left, right, preferred_element_type=F32)


def nt(left, right):
    return lax.dot_general(left, right, (((1,), (1,)), ((), ())), preferred_element_type=F32)


def fold(value):
    half = value.shape[1] // 2
    return jnp.concatenate([value[:, :half], value[:, half:]], axis=0)


def unfold(value):
    return jnp.concatenate([value[:PART], value[PART:]], axis=1)


def slab(rows, k, first=0, count=ROWS):
    return rows.at[pl.ds(pl.multiple_of(k * ROWS + first, ROWS // 2), count)]


def total(into, first, count):
    summed = into[first].astype(F32)
    for index in range(first + 1, first + count):
        summed = summed + into[index].astype(F32)
    return summed


def kernel(
    leaf_source_hbm,
    leaf_noise_hbm,
    sep_source_hbm,
    sep_noise_hbm,
    leaf_inverse_hbm,
    leaf_coupling_hbm,
    sep_inverse_hbm,
    sep_coupling_hbm,
    sep_length,
    leaf_map_hbm,
    sep_map_hbm,
    leaf_sample,
    sep_sample,
    leaf_source,
    leaf_noise,
    sep_source,
    sep_noise,
    leaf_inverse,
    leaf_coupling,
    sep_inverse,
    sep_coupling,
    leaf_map,
    sep_map,
    load_sems,
    sep_rows,
    leaf_rows,
    turned,
    sep_columns,
    leaf_rs_out,
    leaf_rs_in,
    leaf_up_out,
    leaf_up_in,
    sep_rs_out,
    sep_rs_in,
    low_up_out,
    low_up_in,
    parts_out,
    parts_in,
    sep_up_out,
    sep_up_in,
    down_out,
    down_in,
    out_out,
    out_in,
    sample_in,
    leaf_residual_in,
    source_in,
    wanted_out,
    wanted_in,
    solved,
    send_sems,
    recv_sems,
):
    loads = [
        pltpu.make_async_copy(source, target, load_sems.at[index])
        for index, (source, target) in enumerate(
            (
                (leaf_source_hbm, leaf_source),
                (leaf_inverse_hbm, leaf_inverse),
                (leaf_map_hbm, leaf_map),
                (leaf_coupling_hbm, leaf_coupling),
                (sep_map_hbm, sep_map),
                (sep_coupling_hbm, sep_coupling),
                (sep_inverse_hbm, sep_inverse),
                (sep_source_hbm, sep_source),
                (sep_noise_hbm, sep_noise),
                (leaf_noise_hbm, leaf_noise),
            )
        )
    ]
    for load in loads:
        load.start()
    m = lax.axis_index("leaf")
    p = lax.axis_index("panel")
    z = lax.div(p, SIDE)
    y = lax.rem(p, SIDE)
    core = lax.rem(m, 2)
    even = core == 0
    odd = core == 1
    second = lax.rem(m, 4) == 1
    third = m == 3
    top = m == 7
    inner = jnp.logical_or(second, third)

    def step(value, by):
        return lax.rem(value + by, SIDE)

    zs = [step(z, by) * SIDE for by in range(SIDE)]
    ys = [step(y, by) for by in range(SIDE)]
    order = [(2, 2), (2, 1), (2, 3), (1, 2), (3, 2), (1, 1), (1, 3), (3, 1), (3, 3)]
    order += [(0, 2), (2, 0), (0, 1), (0, 3), (1, 0), (3, 0)]
    others = [zs[dz] + ys[dy] for dz, dy in order]
    row = [zs[0] + ys[by] for by in (2, 1, 3, 0)]

    def copy(source, target, kind, leaf, panel):
        pltpu.make_async_remote_copy(
            src_ref=source,
            dst_ref=target,
            send_sem=send_sems.at[kind],
            recv_sem=recv_sems.at[kind],
            device_id=(leaf, panel),
            device_id_type=MESH,
        ).start()

    spans = {4: source_in, 8: leaf_up_in, 16: sep_up_in.at[0], 128: sep_columns}

    def settle(sem, size, count):
        span = spans[size].at[pl.ds(0, count)]
        pltpu.make_async_copy(span, span, sem).wait()

    def arrive(kind, size, count):
        settle(recv_sems.at[kind], size, count)

    def sent(kind, size, count):
        settle(send_sems.at[kind], size, count)

    def mapped(coupling, targets, out):
        row = lax.broadcasted_iota(jnp.int32, (MAP_TILE, ROWS), 0).astype(jnp.int16)
        row = jnp.concatenate([row] * (WIDTH // ROWS), axis=1)
        one = jnp.ones((MAP_TILE, WIDTH), BF16)

        def body(tile, carry):
            first = pl.multiple_of(tile * MAP_TILE, MAP_TILE)
            target = jnp.broadcast_to(targets[...] - first, (MAP_TILE, WIDTH)).astype(jnp.int16)
            chosen = jnp.where(row == target, one, jnp.zeros_like(one))
            out[:, pl.ds(first, MAP_TILE)] = nt(chosen, coupling[0]).T.astype(BF16)
            return carry

        lax.fori_loop(0, WIDTH // MAP_TILE, body, 0)

    barrier = pltpu.get_barrier_semaphore()

    def greet(leaf, panel):
        pl.semaphore_signal(barrier, inc=1, device_id=(leaf, panel), device_id_type=MESH)

    def greet_front(leaf):
        for q in row:
            greet(leaf, q)

    @pl.when(lax.rem(m, 4) == 2)
    def _():
        for q in others + [p]:
            greet(m - 1, q)

    @pl.when(second)
    def _():
        for q in others + [p]:
            greet(m + 1, q)
        greet_front(3)

    @pl.when(third)
    def _():
        greet_front(1)
        greet_front(5)
        greet_front(7)

    @pl.when(top)
    def _():
        greet_front(3)

    twin = m + 1 - 2 * core
    for q in others:
        greet(m, q)
        greet(twin, q)
    greet(twin, p)

    for load in loads[:2]:
        load.wait()
    leaf_partial = nn(leaf_source[...].astype(BF16), leaf_inverse[0])
    for q in range(PANELS):
        leaf_rs_out[q] = leaf_partial[:, q * ROWS : (q + 1) * ROWS].astype(BF16)
    leaf_rs_in[p] = leaf_rs_out[p]
    def prepare():
        for load in loads[4:8]:
            load.wait()
        mapped(sep_coupling, sep_map, slab(sep_rows, z))
        length = sep_length[0]
        row_live = lax.broadcasted_iota(jnp.int32, (ROWS, WIDTH), 0) + p * ROWS < length
        column_live = lax.broadcasted_iota(jnp.int32, (ROWS, WIDTH), 1) < length
        live = jnp.where(jnp.logical_and(row_live, column_live), 1.0, 0.0)
        sep_inverse[0] = sep_inverse[0] * live.astype(BF16)

    def mine(value_ref):
        return value_ref[pl.ds(pl.multiple_of(z * PART, PART), PART), :]

    @pl.when(odd)
    def _():
        prepare()
        for group in range(SIDE):
            for k in range(SIDE):
                first = (k * SIDE + group) * ROWS
                turned[group, :, k * ROWS : (k + 1) * ROWS] = sep_inverse[0, :, first : first + ROWS]
        sep_columns[p] = turned[y]
        source_in[p] = mine(sep_source)

    for load in loads[2:4] + loads[8:]:
        load.wait()

    def rows_near():
        part = slab(sep_rows, z)
        for by in (1, 3):
            copy(part, part, M_NEAR, m, zs[by] + y)

    def rows_far():
        arrive(M_NEAR, 128, 8)
        for by, first in ((1, 0), (3, ROWS // 2)):
            part = slab(sep_rows, step(z, 4 - by), first, ROWS // 2)
            copy(part, part, M_FAR, m, zs[by] + y)

    def columns_turn():
        for by in (2, 1, 3):
            copy(turned.at[ys[by]], sep_columns.at[p], I_TURN, m, zs[0] + ys[by])

    def columns_near():
        arrive(I_TURN, 128, 3)
        part = sep_columns.at[pl.ds(zs[0], SIDE)]
        for by in (1, 3):
            copy(part, part, I_NEAR, m, zs[by] + y)

    def columns_far():
        arrive(I_NEAR, 128, 8)
        for by, first in ((1, 0), (3, 2)):
            part = sep_columns.at[pl.ds(zs[4 - by] + first, 2)]
            copy(part, part, I_FAR, m, zs[by] + y)

    def spread(out, into, base, kind, leaf, own):
        for q in others:
            copy(out.at[q], into.at[base + p], kind, leaf, q)
        if own:
            into[base + p] = out[p]
        else:
            copy(out.at[p], into.at[base + p], kind, leaf, p)

    def cut_columns(value, out):
        for q in range(PANELS):
            out[q] = value[:, q * ROWS : (q + 1) * ROWS].astype(BF16)

    def cut_parts(value, out):
        for split in range(SIDE):
            rows = value[split * PART : (split + 1) * PART]
            for group in range(SIDE):
                firsts = [(k * SIDE + group) * ROWS for k in range(SIDE)]
                chunk = jnp.concatenate([rows[:, first : first + ROWS] for first in firsts], axis=1)
                out[split * SIDE + group] = fold(chunk).astype(BF16)

    def joined_columns(into):
        return jnp.concatenate([into[q] for q in range(PANELS)], axis=1)

    def joined_parts(into):
        pieces = [unfold(into[q].astype(F32)) for q in range(PANELS)]
        blocks = []
        for q in range(PANELS):
            k, group = q // SIDE, q % SIDE
            cut = [pieces[split * SIDE + group][:, k * ROWS : (k + 1) * ROWS] for split in range(SIDE)]
            blocks.append(jnp.concatenate(cut, axis=0).astype(BF16))
        return jnp.concatenate(blocks, axis=1)

    @pl.when(lax.rem(m, 4) == 0)
    def _():
        pl.semaphore_wait(barrier, 31)

    @pl.when(lax.rem(m, 4) == 2)
    def _():
        pl.semaphore_wait(barrier, 47)

    @pl.when(top)
    def _():
        pl.semaphore_wait(barrier, 35)

    @pl.when(second)
    def _():
        pl.semaphore_wait(barrier, 51)

    @pl.when(third)
    def _():
        pl.semaphore_wait(barrier, 43)

    for q in others:
        copy(leaf_rs_out.at[q], leaf_rs_in.at[p], LEAF_RS, m, q)

    @pl.when(odd)
    def _():
        columns_turn()
        rows_near()
        for by in (2, 1, 3):
            part = sep_noise.at[pl.ds(pl.multiple_of(step(z, by) * PART, PART), PART)]
            copy(part, wanted_in.at[z], NOISE, m, zs[by] + y)
        wanted_in[z] = mine(sep_noise)

    @pl.when(jnp.logical_or(third, top))
    def _():
        for dz, dy in order:
            part = sep_source.at[pl.ds(pl.multiple_of(step(z, dz) * PART, PART), PART)]
            copy(part, source_in.at[p], SOURCE, m, zs[dz] + ys[dy])

    mapped(leaf_coupling, leaf_map, leaf_rows)
    arrive(LEAF_RS, 8, 15)
    leaf_solved = total(leaf_rs_in, 0, PANELS)
    cut_columns(nn(leaf_solved.astype(BF16), leaf_rows[...]), leaf_up_out)

    @pl.when(even)
    def _():
        spread(leaf_up_out, leaf_up_in, 0, LEAF_UP, m, True)

    @pl.when(odd)
    def _():
        spread(leaf_up_out, leaf_up_in, PANELS, LEAF_UP, m - 1, False)

    low_parent = jnp.where(lax.rem(m, 4) == 0, m + 1, m - 1)
    low_slot = jnp.where(lax.rem(m, 4) == 0, 0, PANELS)

    @pl.when(even)
    def _():
        prepare()
        arrive(LEAF_UP, 8, 31)
        pending = total(leaf_up_in, 0, 2 * PANELS)
        cut_columns(nn((sep_source[...] - pending).astype(BF16), sep_inverse[0]), sep_rs_out)
        spread(sep_rs_out, sep_rs_in, 0, SEP_RS, m, True)
        arrive(SEP_RS, 8, 15)
        low_solved = total(sep_rs_in, 0, PANELS)
        cut_columns(nn(low_solved.astype(BF16), slab(sep_rows, z)[...]), low_up_out)
        spread(low_up_out, low_up_in, low_slot, LOW_UP, low_parent, False)
        wanted_out[...] = low_solved + sep_noise[...]
        wanted_in[z] = mine(wanted_out)
        for by in (2, 1, 3):
            part = wanted_out.at[pl.ds(pl.multiple_of(step(z, by) * PART, PART), PART)]
            copy(part, wanted_in.at[z], WANTED, m, zs[by] + y)
        rows_near()
        rows_far()
        arrive(M_FAR, 128, 4)
        arrive(WANTED, 4, 3)

    def columns_half(half):
        return sep_columns[half * PANELS // HALVES : (half + 1) * PANELS // HALVES].reshape(HALF, GROUP)

    def front_forward(count):
        found = jnp.zeros((PART, GROUP), F32)
        for half in range(HALVES):
            arrive(SEP_UP + half, 16, count)
            pending = unfold(total(sep_up_in.at[half], 0, count))
            firsts = range(half * PANELS // HALVES, (half + 1) * PANELS // HALVES)
            source = jnp.concatenate([source_in[q] for q in firsts], axis=1)
            found = found + nn((source - pending).astype(BF16), columns_half(half))
        solved[...] = found

    @pl.when(odd)
    def _():
        columns_near()
        rows_far()
        columns_far()
        arrive(M_FAR, 128, 4)
        arrive(NOISE, 4, 3)

    @pl.when(jnp.logical_or(third, top))
    def _():
        arrive(SOURCE, 4, 15)
        arrive(I_FAR, 128, 4)

    @pl.when(second)
    def _():
        arrive(LOW_UP, 8, 32)
        pending = total(low_up_in, 0, 2 * PANELS)
        cut_parts(nn((sep_source[...] - pending).astype(BF16), sep_inverse[0]), parts_out)
        spread(parts_out, parts_in, 0, SEP_RS, m, True)
        arrive(SEP_RS, 8, 15)
        solved[...] = unfold(total(parts_in, 0, PANELS))

    @pl.when(third)
    def _():
        front_forward(8)

    @pl.when(top)
    def _():
        front_forward(4)

    slot = jnp.where(m == 5, SIDE, 0) + y
    parent = jnp.where(third, 7, 3)

    @pl.when(inner)
    def _():
        front = solved[...].astype(BF16)
        for half in range(HALVES):
            update = nn(front, sep_rows[:, half * HALF : (half + 1) * HALF])
            sep_up_out[half] = fold(update).astype(BF16)
            for q in row:
                copy(sep_up_out.at[half], sep_up_in.at[half, slot], SEP_UP + half, parent, q)

    @pl.when(second)
    def _():
        arrive(I_FAR, 128, 4)

    @pl.when(odd)
    def _():
        noise = jnp.concatenate([wanted_in[k] for k in range(SIDE)], axis=1)
        solved[...] = solved[...] + noise

    @pl.when(even)
    def _():
        solved[...] = jnp.concatenate([wanted_in[k] for k in range(SIDE)], axis=1)

    def mapped_back(into, kind, rows, count):
        found = jnp.zeros((PART, GROUP), F32)
        for half in range(HALVES):
            arrive(kind + half, 16, count)
            view = unfold(total(into.at[half], 0, SIDE)).astype(BF16)
            found = found + nt(view, rows[:, half * HALF : (half + 1) * HALF])
        return found

    @pl.when(jnp.logical_not(top))
    def _():
        solved[...] = solved[...] - mapped_back(down_in, DOWN, sep_rows, SIDE)

    residual = solved[...].astype(BF16)

    @pl.when(odd)
    def _():
        for half in range(HALVES):
            sample = nt(residual, columns_half(half))
            down_out[half] = fold(sample).astype(BF16)
            part = down_out.at[half]

            def descend(leaf):
                for q in row:
                    copy(part, down_in.at[half, y], DOWN + half, leaf, q)

            @pl.when(top)
            def _():
                descend(3)

            @pl.when(third)
            def _():
                descend(1)
                descend(5)

            @pl.when(second)
            def _():
                descend(m + 1)
                descend(m - 1)

            for q in range(PANELS // HALVES):
                out_out[half * PANELS // HALVES + q] = sample[:, q * ROWS : (q + 1) * ROWS]

        spread(out_out, out_in, 0, OUT, m, True)
        arrive(OUT, 4, 15)
        for split in range(SIDE):
            sep_sample[split * PART : (split + 1) * PART, :] = total(out_in, split * SIDE, SIDE)
        arrive(SAMPLE, 8, 16)

    @pl.when(even)
    def _():
        parts_in[p] = fold(solved[...]).astype(BF16)
        for q in others:
            copy(parts_in.at[p], parts_in.at[p], SEP_RES, m, q)
        arrive(SEP_RES, 8, 15)
        sample = nt(joined_parts(parts_in), sep_inverse[0])
        sample_in[p] = sample.astype(BF16)
        for q in others:
            copy(sample_in.at[p], sample_in.at[p], SAMPLE, m, q)
            copy(sample_in.at[p], sample_in.at[p], SAMPLE, m + 1, q)
        copy(sample_in.at[p], sample_in.at[p], SAMPLE, m + 1, p)
        sep_sample[...] = sample
        arrive(SAMPLE, 8, 15)

    correction = nt(joined_columns(sample_in), leaf_rows[...])
    leaf_residual_in[p] = (leaf_solved + leaf_noise[...] - correction).astype(BF16)
    for q in others:
        copy(leaf_residual_in.at[p], leaf_residual_in.at[p], LEAF_RES, m, q)
    arrive(LEAF_RES, 8, 15)
    leaf_sample[...] = nt(joined_columns(leaf_residual_in), leaf_inverse[0])

    sent(LEAF_RS, 8, 15)
    sent(LEAF_RES, 8, 15)
    sent(M_NEAR, 128, 8)
    sent(M_FAR, 128, 4)

    @pl.when(even)
    def _():
        sent(LEAF_UP, 8, 15)
        sent(SEP_RS, 8, 15)
        sent(LOW_UP, 8, 16)
        sent(WANTED, 4, 3)
        sent(SEP_RES, 8, 15)
        sent(SAMPLE, 8, 31)

    @pl.when(odd)
    def _():
        sent(LEAF_UP, 8, 16)
        sent(NOISE, 4, 3)
        sent(I_TURN, 128, 3)
        sent(I_NEAR, 128, 8)
        sent(I_FAR, 128, 4)
        sent(OUT, 4, 15)

    @pl.when(jnp.logical_or(third, top))
    def _():
        sent(SOURCE, 4, 15)

    @pl.when(second)
    def _():
        sent(SEP_RS, 8, 15)

    @pl.when(inner)
    def _():
        for half in range(HALVES):
            sent(SEP_UP + half, 16, 4)
            sent(DOWN + half, 16, 8)

    @pl.when(top)
    def _():
        for half in range(HALVES):
            sent(DOWN + half, 16, 4)


def shards(*arrays):
    vmem = pl.BlockSpec(memory_space=pltpu.VMEM)
    hbm = pl.BlockSpec(memory_space=pl.ANY)
    share = jax.ShapeDtypeStruct((SAMPLES, ROWS), F32)
    vector = pltpu.VMEM((SAMPLES, ROWS), F32)
    block = pltpu.VMEM((1, ROWS, WIDTH), BF16)
    targets = pltpu.VMEM((1, WIDTH), jnp.int32)
    slots = pltpu.VMEM((PANELS, SAMPLES, ROWS), BF16)
    pair = pltpu.VMEM((2 * PANELS, SAMPLES, ROWS), BF16)
    split = pltpu.VMEM((PANELS, 2 * PART, GROUP // 2), BF16)
    rows = pltpu.VMEM((GROUP, WIDTH), BF16)
    partial = (2 * PART, HALF // 2)
    pieces = pltpu.VMEM((PANELS, PART, ROWS), F32)
    ring = pltpu.VMEM((SIDE, PART, ROWS), F32)
    return pl.pallas_call(
        kernel,
        out_shape=(share, share),
        in_specs=[hbm] * 8 + [pl.BlockSpec(memory_space=pltpu.SMEM)] + [hbm] * 2,
        out_specs=(vmem, vmem),
        scratch_shapes=[vector] * 4
        + [block] * 4
        + [targets] * 2
        + [pltpu.SemaphoreType.DMA((10,))]
        + [rows, pltpu.VMEM((ROWS, WIDTH), BF16)]
        + [pltpu.VMEM((SIDE, ROWS, GROUP), BF16), pltpu.VMEM((PANELS, ROWS, GROUP), BF16)]
        + [slots, slots, slots, pair]
        + [slots, slots, slots, pair]
        + [split, split]
        + [pltpu.VMEM((HALVES,) + partial, BF16), pltpu.VMEM((HALVES, 2 * SIDE) + partial, BF16)]
        + [pltpu.VMEM((HALVES,) + partial, BF16), pltpu.VMEM((HALVES, SIDE) + partial, BF16)]
        + [pieces, pieces]
        + [slots, slots]
        + [pieces, vector, ring, pltpu.VMEM((PART, GROUP), F32)]
        + [pltpu.SemaphoreType.DMA((KINDS,)), pltpu.SemaphoreType.DMA((KINDS,))],
        compiler_params=pltpu.CompilerParams(
            collective_id=0, has_side_effects=True, vmem_limit_bytes=60 * 1024 * 1024
        ),
    )(*arrays)


def solution(mesh):
    in_specs = (
        P(None, ("leaf", "panel")),
        P(None, ("leaf", "panel")),
        P(None, ("leaf", "panel")),
        P(None, ("leaf", "panel")),
        P("leaf", "panel", None),
        P("leaf", "panel", None),
        P("leaf", "panel", None),
        P("leaf", "panel", None),
        P("leaf"),
        P("leaf", None),
        P("leaf", None),
    )
    out_specs = (P(None, ("leaf", "panel")), P(None, ("leaf", "panel")))
    return jax.shard_map(shards, mesh=mesh, in_specs=in_specs, out_specs=out_specs, check_vma=False)
```

```python
import jax
import jax.numpy as jnp
from jax import lax
from jax.experimental import pallas as pl
from jax.experimental.pallas import tpu as pltpu
from jax.sharding import PartitionSpec as P

MESH = pl.DeviceIdType.MESH
BF16 = jnp.bfloat16
F32 = jnp.float32
PANELS = 16
SIDE = 4
ROWS = 128
GROUP = SIDE * ROWS
WIDTH = 2048
SAMPLES = 32
PART = 8
MAP_TILE = 256
HALVES = 4
HALF = WIDTH // HALVES
LEAF_RS, LEAF_UP, SEP_RS, LOW_UP, OUT, LEAF_RES, NOISE, SOURCE, WANTED, SEP_RES, SAMPLE = range(11)
M_NEAR, M_FAR, I_TURN, I_NEAR, I_FAR = range(11, 16)
SEP_UP, DOWN = range(16, 24, HALVES)
KINDS = 24


def nn(left, right):
    return jnp.dot(left, right, preferred_element_type=F32)


def nt(left, right):
    return lax.dot_general(left, right, (((1,), (1,)), ((), ())), preferred_element_type=F32)


def fold(value):
    half = value.shape[1] // 2
    return jnp.concatenate([value[:, :half], value[:, half:]], axis=0)


def unfold(value):
    return jnp.concatenate([value[:PART], value[PART:]], axis=1)


def slab(rows, k, first=0, count=ROWS):
    return rows.at[pl.ds(pl.multiple_of(k * ROWS + first, ROWS // 2), count)]


def total(into, first, count):
    summed = into[first].astype(F32)
    for index in range(first + 1, first + count):
        summed = summed + into[index].astype(F32)
    return summed


def kernel(
    leaf_source_hbm,
    leaf_noise_hbm,
    sep_source_hbm,
    sep_noise_hbm,
    leaf_inverse_hbm,
    leaf_coupling_hbm,
    sep_inverse_hbm,
    sep_coupling_hbm,
    sep_length,
    leaf_map_hbm,
    sep_map_hbm,
    leaf_sample,
    sep_sample,
    leaf_source,
    leaf_noise,
    sep_source,
    sep_noise,
    leaf_inverse,
    leaf_coupling,
    sep_inverse,
    sep_coupling,
    leaf_map,
    sep_map,
    load_sems,
    sep_rows,
    leaf_rows,
    turned,
    sep_columns,
    leaf_rs_out,
    leaf_rs_in,
    leaf_up_out,
    leaf_up_in,
    sep_rs_out,
    sep_rs_in,
    low_up_out,
    low_up_in,
    parts_out,
    parts_in,
    sep_up_out,
    sep_up_in,
    down_out,
    down_in,
    out_out,
    out_in,
    sample_in,
    leaf_residual_in,
    source_in,
    wanted_out,
    wanted_in,
    solved,
    send_sems,
    recv_sems,
):
    loads = [
        pltpu.make_async_copy(source, target, load_sems.at[index])
        for index, (source, target) in enumerate(
            (
                (leaf_source_hbm, leaf_source),
                (leaf_inverse_hbm, leaf_inverse),
                (leaf_map_hbm, leaf_map),
                (leaf_coupling_hbm, leaf_coupling),
                (sep_map_hbm, sep_map),
                (sep_coupling_hbm, sep_coupling),
                (sep_inverse_hbm, sep_inverse),
                (sep_source_hbm, sep_source),
                (sep_noise_hbm, sep_noise),
                (leaf_noise_hbm, leaf_noise),
            )
        )
    ]
    for load in loads:
        load.start()
    m = lax.axis_index("leaf")
    p = lax.axis_index("panel")
    z = lax.div(p, SIDE)
    y = lax.rem(p, SIDE)
    core = lax.rem(m, 2)
    even = core == 0
    odd = core == 1
    second = lax.rem(m, 4) == 1
    third = m == 3
    top = m == 7
    inner = jnp.logical_or(second, third)

    def step(value, by):
        return lax.rem(value + by, SIDE)

    zs = [step(z, by) * SIDE for by in range(SIDE)]
    ys = [step(y, by) for by in range(SIDE)]
    order = [(2, 2), (2, 1), (2, 3), (1, 2), (3, 2), (1, 1), (1, 3), (3, 1), (3, 3)]
    order += [(0, 2), (2, 0), (0, 1), (0, 3), (1, 0), (3, 0)]
    others = [zs[dz] + ys[dy] for dz, dy in order]
    row = [zs[0] + ys[by] for by in (2, 1, 3, 0)]

    def copy(source, target, kind, leaf, panel):
        pltpu.make_async_remote_copy(
            src_ref=source,
            dst_ref=target,
            send_sem=send_sems.at[kind],
            recv_sem=recv_sems.at[kind],
            device_id=(leaf, panel),
            device_id_type=MESH,
        ).start()

    spans = {4: source_in, 8: leaf_up_in, 16: sep_up_in.at[0], 128: sep_columns}

    def settle(sem, size, count):
        span = spans[size].at[pl.ds(0, count)]
        pltpu.make_async_copy(span, span, sem).wait()

    def arrive(kind, size, count):
        settle(recv_sems.at[kind], size, count)

    def sent(kind, size, count):
        settle(send_sems.at[kind], size, count)

    def mapped(coupling, targets, out):
        row = lax.broadcasted_iota(jnp.int32, (MAP_TILE, ROWS), 0).astype(jnp.int16)
        row = jnp.concatenate([row] * (WIDTH // ROWS), axis=1)
        one = jnp.ones((MAP_TILE, WIDTH), BF16)

        def body(tile, carry):
            first = pl.multiple_of(tile * MAP_TILE, MAP_TILE)
            target = jnp.broadcast_to(targets[...] - first, (MAP_TILE, WIDTH)).astype(jnp.int16)
            chosen = jnp.where(row == target, one, jnp.zeros_like(one))
            out[:, pl.ds(first, MAP_TILE)] = nt(chosen, coupling[0]).T.astype(BF16)
            return carry

        lax.fori_loop(0, WIDTH // MAP_TILE, body, 0)

    barrier = pltpu.get_barrier_semaphore()

    def greet(leaf, panel):
        pl.semaphore_signal(barrier, inc=1, device_id=(leaf, panel), device_id_type=MESH)

    def greet_front(leaf):
        for q in row:
            greet(leaf, q)

    @pl.when(lax.rem(m, 4) == 2)
    def _():
        for q in others + [p]:
            greet(m - 1, q)

    @pl.when(second)
    def _():
        for q in others + [p]:
            greet(m + 1, q)
        greet_front(3)

    @pl.when(third)
    def _():
        greet_front(1)
        greet_front(5)
        greet_front(7)

    @pl.when(top)
    def _():
        greet_front(3)

    twin = m + 1 - 2 * core
    for q in others:
        greet(m, q)
        greet(twin, q)
    greet(twin, p)

    for load in loads[:2]:
        load.wait()
    leaf_partial = nn(leaf_source[...].astype(BF16), leaf_inverse[0])
    for q in range(PANELS):
        leaf_rs_out[q] = leaf_partial[:, q * ROWS : (q + 1) * ROWS].astype(BF16)
    leaf_rs_in[p] = leaf_rs_out[p]
    def prepare():
        for load in loads[4:8]:
            load.wait()
        mapped(sep_coupling, sep_map, slab(sep_rows, z))
        length = sep_length[0]
        row_live = lax.broadcasted_iota(jnp.int32, (ROWS, WIDTH), 0) + p * ROWS < length
        column_live = lax.broadcasted_iota(jnp.int32, (ROWS, WIDTH), 1) < length
        live = jnp.where(jnp.logical_and(row_live, column_live), 1.0, 0.0)
        sep_inverse[0] = sep_inverse[0] * live.astype(BF16)

    def mine(value_ref):
        return value_ref[pl.ds(pl.multiple_of(z * PART, PART), PART), :]

    @pl.when(odd)
    def _():
        prepare()
        for group in range(SIDE):
            for k in range(SIDE):
                first = (k * SIDE + group) * ROWS
                turned[group, :, k * ROWS : (k + 1) * ROWS] = sep_inverse[0, :, first : first + ROWS]
        sep_columns[p] = turned[y]
        source_in[p] = mine(sep_source)

    for load in loads[2:4] + loads[8:]:
        load.wait()

    def rows_near(first=0, count=ROWS):
        part = slab(sep_rows, z, first, count)
        for by in (1, 3):
            copy(part, part, M_NEAR, m, zs[by] + y)

    def rows_far():
        arrive(M_NEAR, 128, 8)
        for by, first in ((1, 0), (3, ROWS // 2)):
            part = slab(sep_rows, step(z, 4 - by), first, ROWS // 2)
            copy(part, part, M_FAR, m, zs[by] + y)

    def columns_turn():
        for by in (2, 1, 3):
            copy(turned.at[ys[by]], sep_columns.at[p], I_TURN, m, zs[0] + ys[by])

    def columns_near():
        arrive(I_TURN, 128, 3)
        part = sep_columns.at[pl.ds(zs[0], SIDE)]
        for by in (1, 3):
            copy(part, part, I_NEAR, m, zs[by] + y)

    def columns_far():
        arrive(I_NEAR, 128, 8)
        for by, first in ((1, 0), (3, 2)):
            part = sep_columns.at[pl.ds(zs[4 - by] + first, 2)]
            copy(part, part, I_FAR, m, zs[by] + y)

    def spread(out, into, base, kind, leaf, own):
        for q in others:
            copy(out.at[q], into.at[base + p], kind, leaf, q)
        if own:
            into[base + p] = out[p]
        else:
            copy(out.at[p], into.at[base + p], kind, leaf, p)

    def cut_columns(value, out):
        for q in range(PANELS):
            out[q] = value[:, q * ROWS : (q + 1) * ROWS].astype(BF16)

    def cut_parts(value, out):
        for split in range(SIDE):
            rows = value[split * PART : (split + 1) * PART]
            for group in range(SIDE):
                firsts = [(k * SIDE + group) * ROWS for k in range(SIDE)]
                chunk = jnp.concatenate([rows[:, first : first + ROWS] for first in firsts], axis=1)
                out[split * SIDE + group] = fold(chunk).astype(BF16)

    def joined_columns(into):
        return jnp.concatenate([into[q] for q in range(PANELS)], axis=1)

    def joined_parts(into):
        pieces = [unfold(into[q].astype(F32)) for q in range(PANELS)]
        blocks = []
        for q in range(PANELS):
            k, group = q // SIDE, q % SIDE
            cut = [pieces[split * SIDE + group][:, k * ROWS : (k + 1) * ROWS] for split in range(SIDE)]
            blocks.append(jnp.concatenate(cut, axis=0).astype(BF16))
        return jnp.concatenate(blocks, axis=1)

    @pl.when(lax.rem(m, 4) == 0)
    def _():
        pl.semaphore_wait(barrier, 31)

    @pl.when(lax.rem(m, 4) == 2)
    def _():
        pl.semaphore_wait(barrier, 47)

    @pl.when(top)
    def _():
        pl.semaphore_wait(barrier, 35)

    @pl.when(second)
    def _():
        pl.semaphore_wait(barrier, 51)

    @pl.when(third)
    def _():
        pl.semaphore_wait(barrier, 43)

    for q in others:
        copy(leaf_rs_out.at[q], leaf_rs_in.at[p], LEAF_RS, m, q)

    @pl.when(odd)
    def _():
        columns_turn()
        rows_near(0, ROWS // 2)
        for by in (2, 1, 3):
            part = sep_noise.at[pl.ds(pl.multiple_of(step(z, by) * PART, PART), PART)]
            copy(part, wanted_in.at[z], NOISE, m, zs[by] + y)
        wanted_in[z] = mine(sep_noise)

    @pl.when(jnp.logical_or(third, top))
    def _():
        for dz, dy in order:
            part = sep_source.at[pl.ds(pl.multiple_of(step(z, dz) * PART, PART), PART)]
            copy(part, source_in.at[p], SOURCE, m, zs[dz] + ys[dy])

    mapped(leaf_coupling, leaf_map, leaf_rows)
    arrive(LEAF_RS, 8, 15)
    leaf_solved = total(leaf_rs_in, 0, PANELS)
    cut_columns(nn(leaf_solved.astype(BF16), leaf_rows[...]), leaf_up_out)

    @pl.when(even)
    def _():
        spread(leaf_up_out, leaf_up_in, 0, LEAF_UP, m, True)

    @pl.when(odd)
    def _():
        spread(leaf_up_out, leaf_up_in, PANELS, LEAF_UP, m - 1, False)
        rows_near(ROWS // 2, ROWS // 2)
        columns_near()

    low_parent = jnp.where(lax.rem(m, 4) == 0, m + 1, m - 1)
    low_slot = jnp.where(lax.rem(m, 4) == 0, 0, PANELS)

    @pl.when(even)
    def _():
        prepare()
        arrive(LEAF_UP, 8, 31)
        pending = total(leaf_up_in, 0, 2 * PANELS)
        cut_columns(nn((sep_source[...] - pending).astype(BF16), sep_inverse[0]), sep_rs_out)
        spread(sep_rs_out, sep_rs_in, 0, SEP_RS, m, True)
        arrive(SEP_RS, 8, 15)
        low_solved = total(sep_rs_in, 0, PANELS)
        cut_columns(nn(low_solved.astype(BF16), slab(sep_rows, z)[...]), low_up_out)
        spread(low_up_out, low_up_in, low_slot, LOW_UP, low_parent, False)
        wanted_out[...] = low_solved + sep_noise[...]
        wanted_in[z] = mine(wanted_out)
        for by in (2, 1, 3):
            part = wanted_out.at[pl.ds(pl.multiple_of(step(z, by) * PART, PART), PART)]
            copy(part, wanted_in.at[z], WANTED, m, zs[by] + y)
        arrive(WANTED, 4, 3)
        rows_near()
        rows_far()
        arrive(M_FAR, 128, 4)

    def columns_half(half):
        return sep_columns[half * PANELS // HALVES : (half + 1) * PANELS // HALVES].reshape(HALF, GROUP)

    def front_forward(count):
        found = jnp.zeros((PART, GROUP), F32)
        for half in range(HALVES):
            arrive(SEP_UP + half, 16, count)
            pending = unfold(total(sep_up_in.at[half], 0, count))
            firsts = range(half * PANELS // HALVES, (half + 1) * PANELS // HALVES)
            source = jnp.concatenate([source_in[q] for q in firsts], axis=1)
            found = found + nn((source - pending).astype(BF16), columns_half(half))
        solved[...] = found

    @pl.when(odd)
    def _():
        rows_far()

    @pl.when(jnp.logical_or(third, top))
    def _():
        columns_far()
        arrive(M_FAR, 128, 4)
        arrive(SOURCE, 4, 15)
        arrive(I_FAR, 128, 4)

    @pl.when(second)
    def _():
        arrive(LOW_UP, 8, 32)
        pending = total(low_up_in, 0, 2 * PANELS)
        cut_parts(nn((sep_source[...] - pending).astype(BF16), sep_inverse[0]), parts_out)
        spread(parts_out, parts_in, 0, SEP_RS, m, True)
        columns_far()
        arrive(SEP_RS, 8, 15)
        solved[...] = unfold(total(parts_in, 0, PANELS))
        arrive(M_FAR, 128, 4)

    @pl.when(third)
    def _():
        front_forward(8)

    @pl.when(top)
    def _():
        front_forward(4)

    slot = jnp.where(m == 5, SIDE, 0) + y
    parent = jnp.where(third, 7, 3)

    @pl.when(inner)
    def _():
        front = solved[...].astype(BF16)
        for half in range(HALVES):
            update = nn(front, sep_rows[:, half * HALF : (half + 1) * HALF])
            sep_up_out[half] = fold(update).astype(BF16)
            for q in row:
                copy(sep_up_out.at[half], sep_up_in.at[half, slot], SEP_UP + half, parent, q)

    @pl.when(second)
    def _():
        arrive(I_FAR, 128, 4)

    @pl.when(odd)
    def _():
        arrive(NOISE, 4, 3)
        noise = jnp.concatenate([wanted_in[k] for k in range(SIDE)], axis=1)
        solved[...] = solved[...] + noise

    @pl.when(even)
    def _():
        solved[...] = jnp.concatenate([wanted_in[k] for k in range(SIDE)], axis=1)

    def mapped_back(into, kind, rows, count):
        found = jnp.zeros((PART, GROUP), F32)
        for half in range(HALVES):
            arrive(kind + half, 16, count)
            view = unfold(total(into.at[half], 0, SIDE)).astype(BF16)
            found = found + nt(view, rows[:, half * HALF : (half + 1) * HALF])
        return found

    @pl.when(jnp.logical_not(top))
    def _():
        solved[...] = solved[...] - mapped_back(down_in, DOWN, sep_rows, SIDE)

    residual = solved[...].astype(BF16)

    @pl.when(odd)
    def _():
        for half in range(HALVES):
            sample = nt(residual, columns_half(half))
            down_out[half] = fold(sample).astype(BF16)
            part = down_out.at[half]

            def descend(leaf):
                for q in row:
                    copy(part, down_in.at[half, y], DOWN + half, leaf, q)

            @pl.when(top)
            def _():
                descend(3)

            @pl.when(third)
            def _():
                descend(1)
                descend(5)

            @pl.when(second)
            def _():
                descend(m + 1)
                descend(m - 1)

            for q in range(PANELS // HALVES):
                out_out[half * PANELS // HALVES + q] = sample[:, q * ROWS : (q + 1) * ROWS]

        spread(out_out, out_in, 0, OUT, m, True)
        arrive(OUT, 4, 15)
        for split in range(SIDE):
            sep_sample[split * PART : (split + 1) * PART, :] = total(out_in, split * SIDE, SIDE)
        arrive(SAMPLE, 8, 16)

    @pl.when(even)
    def _():
        parts_in[p] = fold(solved[...]).astype(BF16)
        for q in others:
            copy(parts_in.at[p], parts_in.at[p], SEP_RES, m, q)
        arrive(SEP_RES, 8, 15)
        sample = nt(joined_parts(parts_in), sep_inverse[0])
        sample_in[p] = sample.astype(BF16)
        for q in others:
            copy(sample_in.at[p], sample_in.at[p], SAMPLE, m, q)
            copy(sample_in.at[p], sample_in.at[p], SAMPLE, m + 1, q)
        copy(sample_in.at[p], sample_in.at[p], SAMPLE, m + 1, p)
        sep_sample[...] = sample
        arrive(SAMPLE, 8, 15)

    correction = nt(joined_columns(sample_in), leaf_rows[...])
    leaf_residual_in[p] = (leaf_solved + leaf_noise[...] - correction).astype(BF16)
    for q in others:
        copy(leaf_residual_in.at[p], leaf_residual_in.at[p], LEAF_RES, m, q)
    arrive(LEAF_RES, 8, 15)
    leaf_sample[...] = nt(joined_columns(leaf_residual_in), leaf_inverse[0])

    sent(LEAF_RS, 8, 15)
    sent(LEAF_RES, 8, 15)
    sent(M_NEAR, 128, 8)
    sent(M_FAR, 128, 4)

    @pl.when(even)
    def _():
        sent(LEAF_UP, 8, 15)
        sent(SEP_RS, 8, 15)
        sent(LOW_UP, 8, 16)
        sent(WANTED, 4, 3)
        sent(SEP_RES, 8, 15)
        sent(SAMPLE, 8, 31)

    @pl.when(odd)
    def _():
        sent(LEAF_UP, 8, 16)
        sent(NOISE, 4, 3)
        sent(I_TURN, 128, 3)
        sent(I_NEAR, 128, 8)
        sent(I_FAR, 128, 4)
        sent(OUT, 4, 15)

    @pl.when(jnp.logical_or(third, top))
    def _():
        sent(SOURCE, 4, 15)

    @pl.when(second)
    def _():
        sent(SEP_RS, 8, 15)

    @pl.when(inner)
    def _():
        for half in range(HALVES):
            sent(SEP_UP + half, 16, 4)
            sent(DOWN + half, 16, 8)

    @pl.when(top)
    def _():
        for half in range(HALVES):
            sent(DOWN + half, 16, 4)


def shards(*arrays):
    vmem = pl.BlockSpec(memory_space=pltpu.VMEM)
    hbm = pl.BlockSpec(memory_space=pl.ANY)
    share = jax.ShapeDtypeStruct((SAMPLES, ROWS), F32)
    vector = pltpu.VMEM((SAMPLES, ROWS), F32)
    block = pltpu.VMEM((1, ROWS, WIDTH), BF16)
    targets = pltpu.VMEM((1, WIDTH), jnp.int32)
    slots = pltpu.VMEM((PANELS, SAMPLES, ROWS), BF16)
    pair = pltpu.VMEM((2 * PANELS, SAMPLES, ROWS), BF16)
    split = pltpu.VMEM((PANELS, 2 * PART, GROUP // 2), BF16)
    rows = pltpu.VMEM((GROUP, WIDTH), BF16)
    partial = (2 * PART, HALF // 2)
    pieces = pltpu.VMEM((PANELS, PART, ROWS), F32)
    ring = pltpu.VMEM((SIDE, PART, ROWS), F32)
    return pl.pallas_call(
        kernel,
        out_shape=(share, share),
        in_specs=[hbm] * 8 + [pl.BlockSpec(memory_space=pltpu.SMEM)] + [hbm] * 2,
        out_specs=(vmem, vmem),
        scratch_shapes=[vector] * 4
        + [block] * 4
        + [targets] * 2
        + [pltpu.SemaphoreType.DMA((10,))]
        + [rows, pltpu.VMEM((ROWS, WIDTH), BF16)]
        + [pltpu.VMEM((SIDE, ROWS, GROUP), BF16), pltpu.VMEM((PANELS, ROWS, GROUP), BF16)]
        + [slots, slots, slots, pair]
        + [slots, slots, slots, pair]
        + [split, split]
        + [pltpu.VMEM((HALVES,) + partial, BF16), pltpu.VMEM((HALVES, 2 * SIDE) + partial, BF16)]
        + [pltpu.VMEM((HALVES,) + partial, BF16), pltpu.VMEM((HALVES, SIDE) + partial, BF16)]
        + [pieces, pieces]
        + [slots, slots]
        + [pieces, vector, ring, pltpu.VMEM((PART, GROUP), F32)]
        + [pltpu.SemaphoreType.DMA((KINDS,)), pltpu.SemaphoreType.DMA((KINDS,))],
        compiler_params=pltpu.CompilerParams(
            collective_id=0, has_side_effects=True, vmem_limit_bytes=60 * 1024 * 1024
        ),
    )(*arrays)


def solution(mesh):
    in_specs = (
        P(None, ("leaf", "panel")),
        P(None, ("leaf", "panel")),
        P(None, ("leaf", "panel")),
        P(None, ("leaf", "panel")),
        P("leaf", "panel", None),
        P("leaf", "panel", None),
        P("leaf", "panel", None),
        P("leaf", "panel", None),
        P("leaf"),
        P("leaf", None),
        P("leaf", None),
    )
    out_specs = (P(None, ("leaf", "panel")), P(None, ("leaf", "panel")))
    return jax.shard_map(shards, mesh=mesh, in_specs=in_specs, out_specs=out_specs, check_vma=False)
```

```python
import jax
import jax.numpy as jnp
from jax import lax
from jax.experimental import pallas as pl
from jax.experimental.pallas import tpu as pltpu
from jax.sharding import PartitionSpec as P

MESH = pl.DeviceIdType.MESH
BF16 = jnp.bfloat16
F32 = jnp.float32
PANELS = 16
SIDE = 4
ROWS = 128
GROUP = SIDE * ROWS
WIDTH = 2048
SAMPLES = 32
PART = 8
MAP_TILE = 256
HALVES = 4
HALF = WIDTH // HALVES
LEAF_RS, LEAF_UP, SEP_RS, LOW_UP, OUT, LEAF_RES, NOISE, SOURCE, WANTED, SEP_RES, SAMPLE = range(11)
M_NEAR, M_FAR, I_TURN, I_NEAR, I_FAR = range(11, 16)
SEP_UP, DOWN = range(16, 24, HALVES)
KINDS = 24


def nn(left, right):
    return jnp.dot(left, right, preferred_element_type=F32)


def nt(left, right):
    return lax.dot_general(left, right, (((1,), (1,)), ((), ())), preferred_element_type=F32)


def fold(value):
    half = value.shape[1] // 2
    return jnp.concatenate([value[:, :half], value[:, half:]], axis=0)


def unfold(value):
    return jnp.concatenate([value[:PART], value[PART:]], axis=1)


def slab(rows, k, first=0, count=ROWS):
    return rows.at[pl.ds(pl.multiple_of(k * ROWS + first, ROWS // 2), count)]


def total(into, first, count):
    summed = into[first].astype(F32)
    for index in range(first + 1, first + count):
        summed = summed + into[index].astype(F32)
    return summed


def kernel(
    leaf_source_hbm,
    leaf_noise_hbm,
    sep_source_hbm,
    sep_noise_hbm,
    leaf_inverse_hbm,
    leaf_coupling_hbm,
    sep_inverse_hbm,
    sep_coupling_hbm,
    sep_length_hbm,
    leaf_map_hbm,
    sep_map_hbm,
    samples,
    leaf_source,
    leaf_noise,
    sep_source,
    sep_noise,
    leaf_inverse,
    leaf_coupling,
    sep_inverse,
    sep_coupling,
    leaf_map,
    sep_map,
    sep_length,
    load_sems,
    sep_rows,
    leaf_rows,
    turned,
    sep_columns,
    leaf_rs_out,
    leaf_rs_in,
    leaf_up_out,
    leaf_up_in,
    sep_rs_out,
    sep_rs_in,
    low_up_out,
    low_up_in,
    parts_out,
    parts_in,
    sep_up_out,
    sep_up_in,
    down_out,
    down_in,
    out_out,
    out_in,
    sample_in,
    leaf_residual_in,
    source_in,
    wanted_out,
    wanted_in,
    solved,
    send_sems,
    recv_sems,
):
    loads = [
        pltpu.make_async_copy(source, target, load_sems.at[index])
        for index, (source, target) in enumerate(
            (
                (leaf_source_hbm, leaf_source),
                (leaf_inverse_hbm, leaf_inverse),
                (leaf_map_hbm, leaf_map),
                (leaf_coupling_hbm, leaf_coupling),
                (sep_map_hbm, sep_map),
                (sep_coupling_hbm, sep_coupling),
                (sep_inverse_hbm, sep_inverse),
                (sep_length_hbm, sep_length),
                (sep_source_hbm, sep_source),
                (sep_noise_hbm, sep_noise),
                (leaf_noise_hbm, leaf_noise),
            )
        )
    ]
    for load in loads:
        load.start()
    m = lax.axis_index("leaf")
    p = lax.axis_index("panel")
    z = lax.div(p, SIDE)
    y = lax.rem(p, SIDE)
    core = lax.rem(m, 2)
    even = core == 0
    odd = core == 1
    second = lax.rem(m, 4) == 1
    third = m == 3
    top = m == 7
    inner = jnp.logical_or(second, third)

    def step(value, by):
        return lax.rem(value + by, SIDE)

    zs = [step(z, by) * SIDE for by in range(SIDE)]
    ys = [step(y, by) for by in range(SIDE)]
    order = [(2, 2), (2, 1), (2, 3), (1, 2), (3, 2), (1, 1), (1, 3), (3, 1), (3, 3)]
    order += [(0, 2), (2, 0), (0, 1), (0, 3), (1, 0), (3, 0)]
    others = [zs[dz] + ys[dy] for dz, dy in order]
    row = [zs[0] + ys[by] for by in (2, 1, 3, 0)]

    def copy(source, target, kind, leaf, panel):
        pltpu.make_async_remote_copy(
            src_ref=source,
            dst_ref=target,
            send_sem=send_sems.at[kind],
            recv_sem=recv_sems.at[kind],
            device_id=(leaf, panel),
            device_id_type=MESH,
        ).start()

    spans = {4: source_in, 8: leaf_up_in, 16: sep_up_in.at[0], 128: sep_columns}

    def settle(sem, size, count):
        span = spans[size].at[pl.ds(0, count)]
        pltpu.make_async_copy(span, span, sem).wait()

    def arrive(kind, size, count):
        settle(recv_sems.at[kind], size, count)

    def sent(kind, size, count):
        settle(send_sems.at[kind], size, count)

    def mapped(coupling, targets, out):
        row = lax.broadcasted_iota(jnp.int32, (MAP_TILE, ROWS), 0).astype(jnp.int16)
        row = jnp.concatenate([row] * (WIDTH // ROWS), axis=1)
        one = jnp.ones((MAP_TILE, WIDTH), BF16)

        def body(tile, carry):
            first = pl.multiple_of(tile * MAP_TILE, MAP_TILE)
            target = jnp.broadcast_to(targets[...] - first, (MAP_TILE, WIDTH)).astype(jnp.int16)
            chosen = jnp.where(row == target, one, jnp.zeros_like(one))
            out[:, pl.ds(first, MAP_TILE)] = nt(chosen, coupling[0]).T.astype(BF16)
            return carry

        lax.fori_loop(0, WIDTH // MAP_TILE, body, 0)

    barrier = pltpu.get_barrier_semaphore()

    def greet(leaf, panel):
        pl.semaphore_signal(barrier, inc=1, device_id=(leaf, panel), device_id_type=MESH)

    def greet_front(leaf):
        for q in row:
            greet(leaf, q)

    @pl.when(lax.rem(m, 4) == 2)
    def _():
        for q in others + [p]:
            greet(m - 1, q)

    @pl.when(second)
    def _():
        for q in others + [p]:
            greet(m + 1, q)
        greet_front(3)

    @pl.when(third)
    def _():
        greet_front(1)
        greet_front(5)
        greet_front(7)

    @pl.when(top)
    def _():
        greet_front(3)

    twin = m + 1 - 2 * core
    for q in others:
        greet(m, q)
        greet(twin, q)
    greet(twin, p)

    for load in loads[:2]:
        load.wait()
    leaf_partial = nn(leaf_source[...].astype(BF16), leaf_inverse[0])
    for q in range(PANELS):
        leaf_rs_out[q] = leaf_partial[:, q * ROWS : (q + 1) * ROWS].astype(BF16)
    leaf_rs_in[p] = leaf_rs_out[p]
    def prepare_rows():
        for load in loads[4:6]:
            load.wait()
        mapped(sep_coupling, sep_map, slab(sep_rows, z))

    def prepare_inverse():
        length = sep_length[0]
        row_live = lax.broadcasted_iota(jnp.int32, (ROWS, WIDTH), 0) + p * ROWS < length
        column_live = lax.broadcasted_iota(jnp.int32, (ROWS, WIDTH), 1) < length
        live = jnp.where(jnp.logical_and(row_live, column_live), 1.0, 0.0)
        sep_inverse[0] = sep_inverse[0] * live.astype(BF16)

    def mine(value_ref):
        return value_ref[pl.ds(pl.multiple_of(z * PART, PART), PART), :]

    @pl.when(odd)
    def _():
        prepare_rows()

    for load in loads[2:4] + loads[6:]:
        load.wait()

    def rows_near(first=0, count=ROWS):
        part = slab(sep_rows, z, first, count)
        for by in (1, 3):
            copy(part, part, M_NEAR, m, zs[by] + y)

    def rows_far():
        arrive(M_NEAR, 128, 8)
        for by, first in ((1, 0), (3, ROWS // 2)):
            part = slab(sep_rows, step(z, 4 - by), first, ROWS // 2)
            copy(part, part, M_FAR, m, zs[by] + y)

    def columns_turn():
        for by in (2, 1, 3):
            copy(turned.at[ys[by]], sep_columns.at[p], I_TURN, m, zs[0] + ys[by])

    def columns_near():
        arrive(I_TURN, 128, 3)
        part = sep_columns.at[pl.ds(zs[0], SIDE)]
        for by in (1, 3):
            copy(part, part, I_NEAR, m, zs[by] + y)

    def columns_far():
        arrive(I_NEAR, 128, 8)
        for by, first in ((1, 0), (3, 2)):
            part = sep_columns.at[pl.ds(zs[4 - by] + first, 2)]
            copy(part, part, I_FAR, m, zs[by] + y)

    def spread(out, into, base, kind, leaf, own):
        for q in others:
            copy(out.at[q], into.at[base + p], kind, leaf, q)
        if own:
            into[base + p] = out[p]
        else:
            copy(out.at[p], into.at[base + p], kind, leaf, p)

    def cut_columns(value, out):
        for q in range(PANELS):
            out[q] = value[:, q * ROWS : (q + 1) * ROWS].astype(BF16)

    def cut_parts(value, out):
        for split in range(SIDE):
            rows = value[split * PART : (split + 1) * PART]
            for group in range(SIDE):
                firsts = [(k * SIDE + group) * ROWS for k in range(SIDE)]
                chunk = jnp.concatenate([rows[:, first : first + ROWS] for first in firsts], axis=1)
                out[split * SIDE + group] = fold(chunk).astype(BF16)

    def joined_columns(into):
        return jnp.concatenate([into[q] for q in range(PANELS)], axis=1)

    def joined_parts(into):
        pieces = [unfold(into[q].astype(F32)) for q in range(PANELS)]
        blocks = []
        for q in range(PANELS):
            k, group = q // SIDE, q % SIDE
            cut = [pieces[split * SIDE + group][:, k * ROWS : (k + 1) * ROWS] for split in range(SIDE)]
            blocks.append(jnp.concatenate(cut, axis=0).astype(BF16))
        return jnp.concatenate(blocks, axis=1)

    @pl.when(lax.rem(m, 4) == 0)
    def _():
        pl.semaphore_wait(barrier, 31)

    @pl.when(lax.rem(m, 4) == 2)
    def _():
        pl.semaphore_wait(barrier, 47)

    @pl.when(top)
    def _():
        pl.semaphore_wait(barrier, 35)

    @pl.when(second)
    def _():
        pl.semaphore_wait(barrier, 51)

    @pl.when(third)
    def _():
        pl.semaphore_wait(barrier, 43)

    for q in others:
        copy(leaf_rs_out.at[q], leaf_rs_in.at[p], LEAF_RS, m, q)

    @pl.when(odd)
    def _():
        prepare_inverse()
        for group in range(SIDE):
            for k in range(SIDE):
                first = (k * SIDE + group) * ROWS
                turned[group, :, k * ROWS : (k + 1) * ROWS] = sep_inverse[0, :, first : first + ROWS]
        sep_columns[p] = turned[y]
        source_in[p] = mine(sep_source)
        columns_turn()
        rows_near(0, ROWS // 2)
        for by in (2, 1, 3):
            part = sep_noise.at[pl.ds(pl.multiple_of(step(z, by) * PART, PART), PART)]
            copy(part, wanted_in.at[z], NOISE, m, zs[by] + y)
        wanted_in[z] = mine(sep_noise)

    @pl.when(jnp.logical_or(third, top))
    def _():
        for dz, dy in order:
            part = sep_source.at[pl.ds(pl.multiple_of(step(z, dz) * PART, PART), PART)]
            copy(part, source_in.at[p], SOURCE, m, zs[dz] + ys[dy])

    mapped(leaf_coupling, leaf_map, leaf_rows)
    arrive(LEAF_RS, 8, 15)
    leaf_solved = total(leaf_rs_in, 0, PANELS)
    cut_columns(nn(leaf_solved.astype(BF16), leaf_rows[...]), leaf_up_out)

    @pl.when(even)
    def _():
        spread(leaf_up_out, leaf_up_in, 0, LEAF_UP, m, True)

    @pl.when(odd)
    def _():
        spread(leaf_up_out, leaf_up_in, PANELS, LEAF_UP, m - 1, False)
        rows_near(ROWS // 2, ROWS // 2)
        columns_near()

    low_parent = jnp.where(lax.rem(m, 4) == 0, m + 1, m - 1)
    low_slot = jnp.where(lax.rem(m, 4) == 0, 0, PANELS)

    @pl.when(even)
    def _():
        prepare_rows()
        prepare_inverse()
        arrive(LEAF_UP, 8, 31)
        pending = total(leaf_up_in, 0, 2 * PANELS)
        cut_columns(nn((sep_source[...] - pending).astype(BF16), sep_inverse[0]), sep_rs_out)
        spread(sep_rs_out, sep_rs_in, 0, SEP_RS, m, True)
        arrive(SEP_RS, 8, 15)
        low_solved = total(sep_rs_in, 0, PANELS)
        cut_columns(nn(low_solved.astype(BF16), slab(sep_rows, z)[...]), low_up_out)
        spread(low_up_out, low_up_in, low_slot, LOW_UP, low_parent, False)
        wanted_out[...] = low_solved + sep_noise[...]
        wanted_in[z] = mine(wanted_out)
        for by in (2, 1, 3):
            part = wanted_out.at[pl.ds(pl.multiple_of(step(z, by) * PART, PART), PART)]
            copy(part, wanted_in.at[z], WANTED, m, zs[by] + y)
        arrive(WANTED, 4, 3)
        rows_near()
        rows_far()
        arrive(M_FAR, 128, 4)

    def columns_half(half):
        return sep_columns[half * PANELS // HALVES : (half + 1) * PANELS // HALVES].reshape(HALF, GROUP)

    def front_forward(count):
        found = jnp.zeros((PART, GROUP), F32)
        for half in range(HALVES):
            arrive(SEP_UP + half, 16, count)
            pending = unfold(total(sep_up_in.at[half], 0, count))
            firsts = range(half * PANELS // HALVES, (half + 1) * PANELS // HALVES)
            source = jnp.concatenate([source_in[q] for q in firsts], axis=1)
            found = found + nn((source - pending).astype(BF16), columns_half(half))
        solved[...] = found

    @pl.when(odd)
    def _():
        rows_far()

    @pl.when(jnp.logical_or(third, top))
    def _():
        columns_far()
        arrive(M_FAR, 128, 4)
        arrive(SOURCE, 4, 15)
        arrive(I_FAR, 128, 4)

    @pl.when(second)
    def _():
        arrive(LOW_UP, 8, 32)
        pending = total(low_up_in, 0, 2 * PANELS)
        cut_parts(nn((sep_source[...] - pending).astype(BF16), sep_inverse[0]), parts_out)
        spread(parts_out, parts_in, 0, SEP_RS, m, True)
        columns_far()
        arrive(SEP_RS, 8, 15)
        solved[...] = unfold(total(parts_in, 0, PANELS))
        arrive(M_FAR, 128, 4)

    @pl.when(third)
    def _():
        front_forward(8)

    @pl.when(top)
    def _():
        front_forward(4)

    slot = jnp.where(m == 5, SIDE, 0) + y
    parent = jnp.where(third, 7, 3)

    @pl.when(inner)
    def _():
        front = solved[...].astype(BF16)
        for half in range(HALVES):
            update = nn(front, sep_rows[:, half * HALF : (half + 1) * HALF])
            sep_up_out[half] = fold(update).astype(BF16)
            for q in row:
                copy(sep_up_out.at[half], sep_up_in.at[half, slot], SEP_UP + half, parent, q)

    @pl.when(second)
    def _():
        arrive(I_FAR, 128, 4)

    @pl.when(odd)
    def _():
        arrive(NOISE, 4, 3)
        noise = jnp.concatenate([wanted_in[k] for k in range(SIDE)], axis=1)
        solved[...] = solved[...] + noise

    @pl.when(even)
    def _():
        solved[...] = jnp.concatenate([wanted_in[k] for k in range(SIDE)], axis=1)

    def mapped_back(into, kind, rows, count):
        found = jnp.zeros((PART, GROUP), F32)
        for half in range(HALVES):
            arrive(kind + half, 16, count)
            view = unfold(total(into.at[half], 0, SIDE)).astype(BF16)
            found = found + nt(view, rows[:, half * HALF : (half + 1) * HALF])
        return found

    @pl.when(jnp.logical_not(top))
    def _():
        solved[...] = solved[...] - mapped_back(down_in, DOWN, sep_rows, SIDE)

    residual = solved[...].astype(BF16)

    @pl.when(odd)
    def _():
        for half in range(HALVES):
            sample = nt(residual, columns_half(half))
            down_out[half] = fold(sample).astype(BF16)
            part = down_out.at[half]

            def descend(leaf):
                for q in row:
                    copy(part, down_in.at[half, y], DOWN + half, leaf, q)

            @pl.when(top)
            def _():
                descend(3)

            @pl.when(third)
            def _():
                descend(1)
                descend(5)

            @pl.when(second)
            def _():
                descend(m + 1)
                descend(m - 1)

            for q in range(PANELS // HALVES):
                out_out[half * PANELS // HALVES + q] = sample[:, q * ROWS : (q + 1) * ROWS]

        spread(out_out, out_in, 0, OUT, m, True)
        arrive(OUT, 4, 15)
        for split in range(SIDE):
            samples[1, split * PART : (split + 1) * PART, :] = total(out_in, split * SIDE, SIDE)
        arrive(SAMPLE, 8, 16)

    @pl.when(even)
    def _():
        parts_in[p] = fold(solved[...]).astype(BF16)
        for q in others:
            copy(parts_in.at[p], parts_in.at[p], SEP_RES, m, q)
        arrive(SEP_RES, 8, 15)
        sample = nt(joined_parts(parts_in), sep_inverse[0])
        sample_in[p] = sample.astype(BF16)
        for q in others:
            copy(sample_in.at[p], sample_in.at[p], SAMPLE, m, q)
            copy(sample_in.at[p], sample_in.at[p], SAMPLE, m + 1, q)
        copy(sample_in.at[p], sample_in.at[p], SAMPLE, m + 1, p)
        samples[1] = sample
        arrive(SAMPLE, 8, 15)

    correction = nt(joined_columns(sample_in), leaf_rows[...])
    leaf_residual_in[p] = (leaf_solved + leaf_noise[...] - correction).astype(BF16)
    for q in others:
        copy(leaf_residual_in.at[p], leaf_residual_in.at[p], LEAF_RES, m, q)
    arrive(LEAF_RES, 8, 15)
    samples[0] = nt(joined_columns(leaf_residual_in), leaf_inverse[0])

    sent(LEAF_RS, 8, 15)
    sent(LEAF_RES, 8, 15)
    sent(M_NEAR, 128, 8)
    sent(M_FAR, 128, 4)

    @pl.when(even)
    def _():
        sent(LEAF_UP, 8, 15)
        sent(SEP_RS, 8, 15)
        sent(LOW_UP, 8, 16)
        sent(WANTED, 4, 3)
        sent(SEP_RES, 8, 15)
        sent(SAMPLE, 8, 31)

    @pl.when(odd)
    def _():
        sent(LEAF_UP, 8, 16)
        sent(NOISE, 4, 3)
        sent(I_TURN, 128, 3)
        sent(I_NEAR, 128, 8)
        sent(I_FAR, 128, 4)
        sent(OUT, 4, 15)

    @pl.when(jnp.logical_or(third, top))
    def _():
        sent(SOURCE, 4, 15)

    @pl.when(second)
    def _():
        sent(SEP_RS, 8, 15)

    @pl.when(inner)
    def _():
        for half in range(HALVES):
            sent(SEP_UP + half, 16, 4)
            sent(DOWN + half, 16, 8)

    @pl.when(top)
    def _():
        for half in range(HALVES):
            sent(DOWN + half, 16, 4)


def shards(*arrays):
    vmem = pl.BlockSpec(memory_space=pltpu.VMEM)
    hbm = pl.BlockSpec(memory_space=pl.ANY)
    share = jax.ShapeDtypeStruct((SAMPLES, ROWS), F32)
    vector = pltpu.VMEM((SAMPLES, ROWS), F32)
    block = pltpu.VMEM((1, ROWS, WIDTH), BF16)
    targets = pltpu.VMEM((1, WIDTH), jnp.int32)
    slots = pltpu.VMEM((PANELS, SAMPLES, ROWS), BF16)
    pair = pltpu.VMEM((2 * PANELS, SAMPLES, ROWS), BF16)
    split = pltpu.VMEM((PANELS, 2 * PART, GROUP // 2), BF16)
    rows = pltpu.VMEM((GROUP, WIDTH), BF16)
    partial = (2 * PART, HALF // 2)
    pieces = pltpu.VMEM((PANELS, PART, ROWS), F32)
    ring = pltpu.VMEM((SIDE, PART, ROWS), F32)
    both = pl.pallas_call(
        kernel,
        out_shape=jax.ShapeDtypeStruct((2, SAMPLES, ROWS), F32),
        in_specs=[hbm] * 11,
        out_specs=vmem,
        scratch_shapes=[vector] * 4
        + [block] * 4
        + [targets] * 2
        + [pltpu.SMEM((1,), jnp.int32)]
        + [pltpu.SemaphoreType.DMA((11,))]
        + [rows, pltpu.VMEM((ROWS, WIDTH), BF16)]
        + [pltpu.VMEM((SIDE, ROWS, GROUP), BF16), pltpu.VMEM((PANELS, ROWS, GROUP), BF16)]
        + [slots, slots, slots, pair]
        + [slots, slots, slots, pair]
        + [split, split]
        + [pltpu.VMEM((HALVES,) + partial, BF16), pltpu.VMEM((HALVES, 2 * SIDE) + partial, BF16)]
        + [pltpu.VMEM((HALVES,) + partial, BF16), pltpu.VMEM((HALVES, SIDE) + partial, BF16)]
        + [pieces, pieces]
        + [slots, slots]
        + [pieces, vector, ring, pltpu.VMEM((PART, GROUP), F32)]
        + [pltpu.SemaphoreType.DMA((KINDS,)), pltpu.SemaphoreType.DMA((KINDS,))],
        compiler_params=pltpu.CompilerParams(
            collective_id=0, has_side_effects=True, vmem_limit_bytes=60 * 1024 * 1024
        ),
    )(*arrays)
    return both[0], both[1]


def solution(mesh):
    in_specs = (
        P(None, ("leaf", "panel")),
        P(None, ("leaf", "panel")),
        P(None, ("leaf", "panel")),
        P(None, ("leaf", "panel")),
        P("leaf", "panel", None),
        P("leaf", "panel", None),
        P("leaf", "panel", None),
        P("leaf", "panel", None),
        P("leaf"),
        P("leaf", None),
        P("leaf", None),
    )
    out_specs = (P(None, ("leaf", "panel")), P(None, ("leaf", "panel")))
    return jax.shard_map(shards, mesh=mesh, in_specs=in_specs, out_specs=out_specs, check_vma=False)
```

```python
import jax
import jax.numpy as jnp
from jax import lax
from jax.experimental import pallas as pl
from jax.experimental.pallas import tpu as pltpu
from jax.sharding import PartitionSpec as P

MESH = pl.DeviceIdType.MESH
BF16 = jnp.bfloat16
F32 = jnp.float32
PANELS = 16
SIDE = 4
ROWS = 128
GROUP = SIDE * ROWS
WIDTH = 2048
SAMPLES = 32
PART = 8
MAP_TILE = 256
HALVES = 4
HALF = WIDTH // HALVES
LEAF_RS, LEAF_UP, SEP_RS, LOW_UP, OUT, LEAF_RES, NOISE, SOURCE, WANTED, SEP_RES, SAMPLE = range(11)
M_NEAR, M_FAR, I_TURN, I_NEAR, I_FAR = range(11, 16)
SEP_UP, DOWN = range(16, 24, HALVES)
KINDS = 24


def nn(left, right):
    return jnp.dot(left, right, preferred_element_type=F32)


def nt(left, right):
    return lax.dot_general(left, right, (((1,), (1,)), ((), ())), preferred_element_type=F32)


def fold(value):
    half = value.shape[1] // 2
    return jnp.concatenate([value[:, :half], value[:, half:]], axis=0)


def unfold(value):
    return jnp.concatenate([value[:PART], value[PART:]], axis=1)


def slab(rows, k, first=0, count=ROWS):
    return rows.at[pl.ds(pl.multiple_of(k * ROWS + first, ROWS // 2), count)]


def total(into, first, count):
    summed = into[first].astype(F32)
    for index in range(first + 1, first + count):
        summed = summed + into[index].astype(F32)
    return summed


def kernel(
    leaf_source_hbm,
    leaf_noise_hbm,
    sep_source_hbm,
    sep_noise_hbm,
    leaf_inverse_hbm,
    leaf_coupling_hbm,
    sep_inverse_hbm,
    sep_coupling_hbm,
    sep_length_hbm,
    leaf_map_hbm,
    sep_map_hbm,
    samples,
    leaf_source,
    leaf_noise,
    sep_source,
    sep_noise,
    leaf_inverse,
    leaf_coupling,
    sep_inverse,
    sep_coupling,
    leaf_map,
    sep_map,
    sep_length,
    load_sems,
    sep_rows,
    leaf_rows,
    turned,
    sep_columns,
    leaf_rs_out,
    leaf_rs_in,
    leaf_up_out,
    leaf_up_in,
    sep_rs_out,
    sep_rs_in,
    low_up_out,
    low_up_in,
    parts_out,
    parts_in,
    sep_up_out,
    sep_up_in,
    down_out,
    down_in,
    out_out,
    out_in,
    sample_in,
    leaf_residual_in,
    source_in,
    wanted_out,
    wanted_in,
    solved,
    send_sems,
    recv_sems,
):
    loads = [
        pltpu.make_async_copy(source, target, load_sems.at[index])
        for index, (source, target) in enumerate(
            (
                (leaf_source_hbm, leaf_source),
                (leaf_inverse_hbm, leaf_inverse),
                (leaf_map_hbm, leaf_map),
                (leaf_coupling_hbm, leaf_coupling),
                (sep_map_hbm, sep_map),
                (sep_coupling_hbm, sep_coupling),
                (sep_inverse_hbm, sep_inverse),
                (sep_length_hbm, sep_length),
                (sep_source_hbm, sep_source),
                (sep_noise_hbm, sep_noise),
                (leaf_noise_hbm, leaf_noise),
            )
        )
    ]
    for load in loads:
        load.start()
    m = lax.axis_index("leaf")
    p = lax.axis_index("panel")
    z = lax.div(p, SIDE)
    y = lax.rem(p, SIDE)
    core = lax.rem(m, 2)
    even = core == 0
    odd = core == 1
    second = lax.rem(m, 4) == 1
    third = m == 3
    top = m == 7
    inner = jnp.logical_or(second, third)

    def step(value, by):
        return lax.rem(value + by, SIDE)

    zs = [step(z, by) * SIDE for by in range(SIDE)]
    ys = [step(y, by) for by in range(SIDE)]
    order = [(2, 2), (2, 1), (2, 3), (1, 2), (3, 2), (1, 1), (1, 3), (3, 1), (3, 3)]
    order += [(0, 2), (2, 0), (0, 1), (0, 3), (1, 0), (3, 0)]
    others = [zs[dz] + ys[dy] for dz, dy in order]
    row = [zs[0] + ys[by] for by in (2, 1, 3, 0)]

    def copy(source, target, kind, leaf, panel):
        pltpu.make_async_remote_copy(
            src_ref=source,
            dst_ref=target,
            send_sem=send_sems.at[kind],
            recv_sem=recv_sems.at[kind],
            device_id=(leaf, panel),
            device_id_type=MESH,
        ).start()

    spans = {4: source_in, 8: leaf_up_in, 16: sep_up_in.at[0], 128: sep_columns}

    def settle(sem, size, count):
        span = spans[size].at[pl.ds(0, count)]
        pltpu.make_async_copy(span, span, sem).wait()

    def arrive(kind, size, count):
        settle(recv_sems.at[kind], size, count)

    def sent(kind, size, count):
        settle(send_sems.at[kind], size, count)

    def mapped(coupling, targets, out):
        row = lax.broadcasted_iota(jnp.int32, (MAP_TILE, ROWS), 0).astype(jnp.int16)
        row = jnp.concatenate([row] * (WIDTH // ROWS), axis=1)
        one = jnp.ones((MAP_TILE, WIDTH), BF16)

        def body(tile, carry):
            first = pl.multiple_of(tile * MAP_TILE, MAP_TILE)
            target = jnp.broadcast_to(targets[...] - first, (MAP_TILE, WIDTH)).astype(jnp.int16)
            chosen = jnp.where(row == target, one, jnp.zeros_like(one))
            out[:, pl.ds(first, MAP_TILE)] = nt(chosen, coupling[0]).T.astype(BF16)
            return carry

        lax.fori_loop(0, WIDTH // MAP_TILE, body, 0)

    barrier = pltpu.get_barrier_semaphore()

    def greet(leaf, panel):
        pl.semaphore_signal(barrier, inc=1, device_id=(leaf, panel), device_id_type=MESH)

    def greet_front(leaf):
        for q in row:
            greet(leaf, q)

    @pl.when(lax.rem(m, 4) == 2)
    def _():
        for q in others + [p]:
            greet(m - 1, q)

    @pl.when(second)
    def _():
        for q in others + [p]:
            greet(m + 1, q)
        greet_front(3)

    @pl.when(third)
    def _():
        greet_front(1)
        greet_front(5)
        greet_front(7)

    @pl.when(top)
    def _():
        greet_front(3)

    twin = m + 1 - 2 * core
    for q in others:
        greet(m, q)
        greet(twin, q)
    greet(twin, p)

    for load in loads[:2]:
        load.wait()
    leaf_partial = nn(leaf_source[...].astype(BF16), leaf_inverse[0])
    for q in range(PANELS):
        leaf_rs_out[q] = leaf_partial[:, q * ROWS : (q + 1) * ROWS].astype(BF16)
    leaf_rs_in[p] = leaf_rs_out[p]
    def prepare_rows():
        for load in loads[4:6]:
            load.wait()
        mapped(sep_coupling, sep_map, slab(sep_rows, z))

    def prepare_inverse():
        length = sep_length[0]
        row_live = lax.broadcasted_iota(jnp.int32, (ROWS, WIDTH), 0) + p * ROWS < length
        column_live = lax.broadcasted_iota(jnp.int32, (ROWS, WIDTH), 1) < length
        live = jnp.where(jnp.logical_and(row_live, column_live), 1.0, 0.0)
        sep_inverse[0] = sep_inverse[0] * live.astype(BF16)

    def mine(value_ref):
        return value_ref[pl.ds(pl.multiple_of(z * PART, PART), PART), :]

    for load in loads[2:4] + loads[6:]:
        load.wait()

    def rows_near(first=0, count=ROWS):
        part = slab(sep_rows, z, first, count)
        for by in (1, 3):
            copy(part, part, M_NEAR, m, zs[by] + y)

    def rows_far():
        arrive(M_NEAR, 128, 8)
        for by, first in ((1, 0), (3, ROWS // 2)):
            part = slab(sep_rows, step(z, 4 - by), first, ROWS // 2)
            copy(part, part, M_FAR, m, zs[by] + y)

    def columns_turn():
        for by in (2, 1, 3):
            copy(turned.at[ys[by]], sep_columns.at[p], I_TURN, m, zs[0] + ys[by])

    def columns_near():
        arrive(I_TURN, 128, 3)
        part = sep_columns.at[pl.ds(zs[0], SIDE)]
        for by in (1, 3):
            copy(part, part, I_NEAR, m, zs[by] + y)

    def columns_far():
        arrive(I_NEAR, 128, 8)
        for by, first in ((1, 0), (3, 2)):
            part = sep_columns.at[pl.ds(zs[4 - by] + first, 2)]
            copy(part, part, I_FAR, m, zs[by] + y)

    def spread(out, into, base, kind, leaf, own):
        for q in others:
            copy(out.at[q], into.at[base + p], kind, leaf, q)
        if own:
            into[base + p] = out[p]
        else:
            copy(out.at[p], into.at[base + p], kind, leaf, p)

    def cut_columns(value, out):
        for q in range(PANELS):
            out[q] = value[:, q * ROWS : (q + 1) * ROWS].astype(BF16)

    def cut_parts(value, out):
        for split in range(SIDE):
            rows = value[split * PART : (split + 1) * PART]
            for group in range(SIDE):
                firsts = [(k * SIDE + group) * ROWS for k in range(SIDE)]
                chunk = jnp.concatenate([rows[:, first : first + ROWS] for first in firsts], axis=1)
                out[split * SIDE + group] = fold(chunk).astype(BF16)

    def joined_columns(into):
        return jnp.concatenate([into[q] for q in range(PANELS)], axis=1)

    def joined_parts(into):
        pieces = [unfold(into[q].astype(F32)) for q in range(PANELS)]
        blocks = []
        for q in range(PANELS):
            k, group = q // SIDE, q % SIDE
            cut = [pieces[split * SIDE + group][:, k * ROWS : (k + 1) * ROWS] for split in range(SIDE)]
            blocks.append(jnp.concatenate(cut, axis=0).astype(BF16))
        return jnp.concatenate(blocks, axis=1)

    @pl.when(lax.rem(m, 4) == 0)
    def _():
        pl.semaphore_wait(barrier, 31)

    @pl.when(lax.rem(m, 4) == 2)
    def _():
        pl.semaphore_wait(barrier, 47)

    @pl.when(top)
    def _():
        pl.semaphore_wait(barrier, 35)

    @pl.when(second)
    def _():
        pl.semaphore_wait(barrier, 51)

    @pl.when(third)
    def _():
        pl.semaphore_wait(barrier, 43)

    for q in others:
        copy(leaf_rs_out.at[q], leaf_rs_in.at[p], LEAF_RS, m, q)

    @pl.when(odd)
    def _():
        prepare_inverse()
        for group in range(SIDE):
            for k in range(SIDE):
                first = (k * SIDE + group) * ROWS
                turned[group, :, k * ROWS : (k + 1) * ROWS] = sep_inverse[0, :, first : first + ROWS]
        sep_columns[p] = turned[y]
        source_in[p] = mine(sep_source)
        columns_turn()
        for by in (2, 1, 3):
            part = sep_noise.at[pl.ds(pl.multiple_of(step(z, by) * PART, PART), PART)]
            copy(part, wanted_in.at[z], NOISE, m, zs[by] + y)
        wanted_in[z] = mine(sep_noise)

    @pl.when(jnp.logical_or(third, top))
    def _():
        for dz, dy in order:
            part = sep_source.at[pl.ds(pl.multiple_of(step(z, dz) * PART, PART), PART)]
            copy(part, source_in.at[p], SOURCE, m, zs[dz] + ys[dy])

    mapped(leaf_coupling, leaf_map, leaf_rows)

    @pl.when(odd)
    def _():
        prepare_rows()

    arrive(LEAF_RS, 8, 15)
    leaf_solved = total(leaf_rs_in, 0, PANELS)
    cut_columns(nn(leaf_solved.astype(BF16), leaf_rows[...]), leaf_up_out)

    @pl.when(even)
    def _():
        spread(leaf_up_out, leaf_up_in, 0, LEAF_UP, m, True)

    @pl.when(odd)
    def _():
        spread(leaf_up_out, leaf_up_in, PANELS, LEAF_UP, m - 1, False)
        rows_near()
        columns_near()

    low_parent = jnp.where(lax.rem(m, 4) == 0, m + 1, m - 1)
    low_slot = jnp.where(lax.rem(m, 4) == 0, 0, PANELS)

    @pl.when(even)
    def _():
        prepare_rows()
        prepare_inverse()
        arrive(LEAF_UP, 8, 31)
        pending = total(leaf_up_in, 0, 2 * PANELS)
        cut_columns(nn((sep_source[...] - pending).astype(BF16), sep_inverse[0]), sep_rs_out)
        spread(sep_rs_out, sep_rs_in, 0, SEP_RS, m, True)
        arrive(SEP_RS, 8, 15)
        low_solved = total(sep_rs_in, 0, PANELS)
        cut_columns(nn(low_solved.astype(BF16), slab(sep_rows, z)[...]), low_up_out)
        spread(low_up_out, low_up_in, low_slot, LOW_UP, low_parent, False)
        wanted_out[...] = low_solved + sep_noise[...]
        wanted_in[z] = mine(wanted_out)
        for by in (2, 1, 3):
            part = wanted_out.at[pl.ds(pl.multiple_of(step(z, by) * PART, PART), PART)]
            copy(part, wanted_in.at[z], WANTED, m, zs[by] + y)
        arrive(WANTED, 4, 3)
        rows_near()
        rows_far()
        arrive(M_FAR, 128, 4)

    def columns_half(half):
        return sep_columns[half * PANELS // HALVES : (half + 1) * PANELS // HALVES].reshape(HALF, GROUP)

    def front_forward(count):
        found = jnp.zeros((PART, GROUP), F32)
        for half in range(HALVES):
            arrive(SEP_UP + half, 16, count)
            pending = unfold(total(sep_up_in.at[half], 0, count))
            firsts = range(half * PANELS // HALVES, (half + 1) * PANELS // HALVES)
            source = jnp.concatenate([source_in[q] for q in firsts], axis=1)
            found = found + nn((source - pending).astype(BF16), columns_half(half))
        solved[...] = found

    @pl.when(odd)
    def _():
        rows_far()

    @pl.when(jnp.logical_or(third, top))
    def _():
        columns_far()
        arrive(M_FAR, 128, 4)
        arrive(SOURCE, 4, 15)
        arrive(I_FAR, 128, 4)

    @pl.when(second)
    def _():
        arrive(LOW_UP, 8, 32)
        pending = total(low_up_in, 0, 2 * PANELS)
        cut_parts(nn((sep_source[...] - pending).astype(BF16), sep_inverse[0]), parts_out)
        spread(parts_out, parts_in, 0, SEP_RS, m, True)
        columns_far()
        arrive(SEP_RS, 8, 15)
        solved[...] = unfold(total(parts_in, 0, PANELS))
        arrive(M_FAR, 128, 4)

    @pl.when(third)
    def _():
        front_forward(8)

    @pl.when(top)
    def _():
        front_forward(4)

    slot = jnp.where(m == 5, SIDE, 0) + y
    parent = jnp.where(third, 7, 3)

    @pl.when(inner)
    def _():
        front = solved[...].astype(BF16)
        for half in range(HALVES):
            update = nn(front, sep_rows[:, half * HALF : (half + 1) * HALF])
            sep_up_out[half] = fold(update).astype(BF16)
            for q in row:
                copy(sep_up_out.at[half], sep_up_in.at[half, slot], SEP_UP + half, parent, q)

    @pl.when(second)
    def _():
        arrive(I_FAR, 128, 4)

    @pl.when(odd)
    def _():
        arrive(NOISE, 4, 3)
        noise = jnp.concatenate([wanted_in[k] for k in range(SIDE)], axis=1)
        solved[...] = solved[...] + noise

    @pl.when(even)
    def _():
        solved[...] = jnp.concatenate([wanted_in[k] for k in range(SIDE)], axis=1)

    def mapped_back(into, kind, rows, count):
        found = jnp.zeros((PART, GROUP), F32)
        for half in range(HALVES):
            arrive(kind + half, 16, count)
            view = unfold(total(into.at[half], 0, SIDE)).astype(BF16)
            found = found + nt(view, rows[:, half * HALF : (half + 1) * HALF])
        return found

    @pl.when(jnp.logical_not(top))
    def _():
        solved[...] = solved[...] - mapped_back(down_in, DOWN, sep_rows, SIDE)

    residual = solved[...].astype(BF16)

    @pl.when(odd)
    def _():
        for half in range(HALVES):
            sample = nt(residual, columns_half(half))
            down_out[half] = fold(sample).astype(BF16)
            part = down_out.at[half]

            def descend(leaf):
                for q in row:
                    copy(part, down_in.at[half, y], DOWN + half, leaf, q)

            @pl.when(top)
            def _():
                descend(3)

            @pl.when(third)
            def _():
                descend(1)
                descend(5)

            @pl.when(second)
            def _():
                descend(m + 1)
                descend(m - 1)

            for q in range(PANELS // HALVES):
                out_out[half * PANELS // HALVES + q] = sample[:, q * ROWS : (q + 1) * ROWS]

        spread(out_out, out_in, 0, OUT, m, True)
        arrive(OUT, 4, 15)
        for split in range(SIDE):
            samples[1, split * PART : (split + 1) * PART, :] = total(out_in, split * SIDE, SIDE)
        arrive(SAMPLE, 8, 16)

    @pl.when(even)
    def _():
        parts_in[p] = fold(solved[...]).astype(BF16)
        for q in others:
            copy(parts_in.at[p], parts_in.at[p], SEP_RES, m, q)
        arrive(SEP_RES, 8, 15)
        sample = nt(joined_parts(parts_in), sep_inverse[0])
        sample_in[p] = sample.astype(BF16)
        for q in others:
            copy(sample_in.at[p], sample_in.at[p], SAMPLE, m, q)
            copy(sample_in.at[p], sample_in.at[p], SAMPLE, m + 1, q)
        copy(sample_in.at[p], sample_in.at[p], SAMPLE, m + 1, p)
        samples[1] = sample
        arrive(SAMPLE, 8, 15)

    correction = nt(joined_columns(sample_in), leaf_rows[...])
    leaf_residual_in[p] = (leaf_solved + leaf_noise[...] - correction).astype(BF16)
    for q in others:
        copy(leaf_residual_in.at[p], leaf_residual_in.at[p], LEAF_RES, m, q)
    arrive(LEAF_RES, 8, 15)
    samples[0] = nt(joined_columns(leaf_residual_in), leaf_inverse[0])

    sent(LEAF_RS, 8, 15)
    sent(LEAF_RES, 8, 15)
    sent(M_NEAR, 128, 8)
    sent(M_FAR, 128, 4)

    @pl.when(even)
    def _():
        sent(LEAF_UP, 8, 15)
        sent(SEP_RS, 8, 15)
        sent(LOW_UP, 8, 16)
        sent(WANTED, 4, 3)
        sent(SEP_RES, 8, 15)
        sent(SAMPLE, 8, 31)

    @pl.when(odd)
    def _():
        sent(LEAF_UP, 8, 16)
        sent(NOISE, 4, 3)
        sent(I_TURN, 128, 3)
        sent(I_NEAR, 128, 8)
        sent(I_FAR, 128, 4)
        sent(OUT, 4, 15)

    @pl.when(jnp.logical_or(third, top))
    def _():
        sent(SOURCE, 4, 15)

    @pl.when(second)
    def _():
        sent(SEP_RS, 8, 15)

    @pl.when(inner)
    def _():
        for half in range(HALVES):
            sent(SEP_UP + half, 16, 4)
            sent(DOWN + half, 16, 8)

    @pl.when(top)
    def _():
        for half in range(HALVES):
            sent(DOWN + half, 16, 4)


def shards(*arrays):
    vmem = pl.BlockSpec(memory_space=pltpu.VMEM)
    hbm = pl.BlockSpec(memory_space=pl.ANY)
    share = jax.ShapeDtypeStruct((SAMPLES, ROWS), F32)
    vector = pltpu.VMEM((SAMPLES, ROWS), F32)
    block = pltpu.VMEM((1, ROWS, WIDTH), BF16)
    targets = pltpu.VMEM((1, WIDTH), jnp.int32)
    slots = pltpu.VMEM((PANELS, SAMPLES, ROWS), BF16)
    pair = pltpu.VMEM((2 * PANELS, SAMPLES, ROWS), BF16)
    split = pltpu.VMEM((PANELS, 2 * PART, GROUP // 2), BF16)
    rows = pltpu.VMEM((GROUP, WIDTH), BF16)
    partial = (2 * PART, HALF // 2)
    pieces = pltpu.VMEM((PANELS, PART, ROWS), F32)
    ring = pltpu.VMEM((SIDE, PART, ROWS), F32)
    both = pl.pallas_call(
        kernel,
        out_shape=jax.ShapeDtypeStruct((2, SAMPLES, ROWS), F32),
        in_specs=[hbm] * 11,
        out_specs=vmem,
        scratch_shapes=[vector] * 4
        + [block] * 4
        + [targets] * 2
        + [pltpu.SMEM((1,), jnp.int32)]
        + [pltpu.SemaphoreType.DMA((11,))]
        + [rows, pltpu.VMEM((ROWS, WIDTH), BF16)]
        + [pltpu.VMEM((SIDE, ROWS, GROUP), BF16), pltpu.VMEM((PANELS, ROWS, GROUP), BF16)]
        + [slots, slots, slots, pair]
        + [slots, slots, slots, pair]
        + [split, split]
        + [pltpu.VMEM((HALVES,) + partial, BF16), pltpu.VMEM((HALVES, 2 * SIDE) + partial, BF16)]
        + [pltpu.VMEM((HALVES,) + partial, BF16), pltpu.VMEM((HALVES, SIDE) + partial, BF16)]
        + [pieces, pieces]
        + [slots, slots]
        + [pieces, vector, ring, pltpu.VMEM((PART, GROUP), F32)]
        + [pltpu.SemaphoreType.DMA((KINDS,)), pltpu.SemaphoreType.DMA((KINDS,))],
        compiler_params=pltpu.CompilerParams(
            collective_id=0, has_side_effects=True, vmem_limit_bytes=60 * 1024 * 1024
        ),
    )(*arrays)
    return both[0], both[1]


def solution(mesh):
    in_specs = (
        P(None, ("leaf", "panel")),
        P(None, ("leaf", "panel")),
        P(None, ("leaf", "panel")),
        P(None, ("leaf", "panel")),
        P("leaf", "panel", None),
        P("leaf", "panel", None),
        P("leaf", "panel", None),
        P("leaf", "panel", None),
        P("leaf"),
        P("leaf", None),
        P("leaf", None),
    )
    out_specs = (P(None, ("leaf", "panel")), P(None, ("leaf", "panel")))
    return jax.shard_map(shards, mesh=mesh, in_specs=in_specs, out_specs=out_specs, check_vma=False)
```
